32 devices in a mesh: dp: 4 (over z), head: 2 (over x), ctx: 4 (over y, core).
Axes of the slice: x: 2, y: 2, z: 4, core: 2. Of those that a mesh axis runs over, the one named last changes fastest.
Arguments:
- query_rows: bfloat16 [4096, 8192], P(('dp', 'ctx'), 'head'), parts along dimension 0, may hold values from -12 to 12
- key_rows: bfloat16 [4096, 1024], P(('dp', 'ctx'), 'head'), parts along dimension 0, may hold values from -4 to 4
- stored_value_rows: bfloat16 [4096, 1024], P(('dp', 'ctx'), 'head'), parts along dimension 0, may hold values from -6 to 6
- out_grad: bfloat16 [4096, 8192], P(('dp', 'ctx'), 'head'), parts along dimension 0, may hold values from -6 to 6
- block_table: int32 [16, 2], P('dp'), parts along dimension 0, may hold values from 0 to 7, as said below
- pattern: int32 [32, 10], P('dp'), parts along dimension 0, may hold values from 0 to 7, as said below
Outputs:
- attended: bfloat16 [4096, 8192], P(('dp', 'ctx'), 'head'), parts along dimension 0
- query_grad: bfloat16 [4096, 8192], P(('dp', 'ctx'), 'head'), parts along dimension 0
- key_grad: bfloat16 [4096, 1024], P(('dp', 'ctx'), 'head'), parts along dimension 0
- value_grad: bfloat16 [4096, 1024], P(('dp', 'ctx'), 'head'), parts along dimension 0
The draws below stay inside these ranges and needn't reach their ends.
There are 4 independent parts, one for each index of `dp`. The reference program is written for one: setup_inputs(seed, part) draws one part's arguments, and reference() takes and returns one part's arrays. A program takes and returns all parts, laid end to end along the dimension named above; each array names one. Nothing has to cross between parts.
Inputs may be any that keep to these rules, and one draw needn't show every extreme that they name: `pattern`: row b lists the key blocks that sequence block b reads, in no order; every entry is at most b; b, max(b - 1, 0) and 0 are always listed; repeated entries count once. `block_table`: each sequence block is held by exactly one storage block, and sequence blocks b and 7 - b are held by the same ctx index.
All inputs are finite; a program needn't handle non-finite values.
Results may differ from the reference program's by a relative error of at most 0.015.
Values may be sent and summed in bfloat16 or wider, within the bound.
A program may use at most 128 MiB of HBM per device.

```python
import jax
import jax.numpy as jnp
from jax import lax

QUERY_HEADS = 64
KEY_VALUE_HEADS = 8
HEAD_SIZE = 128
BLK = 128
KMAX = 10
BLK_DEV = 2
SEQUENCE_BLOCKS = 8
EPISODE_TOKENS = 1024
N_CTX = 4


def draw_query_rows(key, part):
    row_count = SEQUENCE_BLOCKS * BLK
    complete_shape = (row_count, KEY_VALUE_HEADS, QUERY_HEADS // KEY_VALUE_HEADS, HEAD_SIZE)
    sampled_values = jnp.clip(jax.random.normal(jax.random.fold_in(key, 11), complete_shape, jnp.float32), -6.0, 6.0)
    return sampled_values.reshape(row_count, QUERY_HEADS * HEAD_SIZE).astype(jnp.bfloat16)


def draw_key_rows(key, part):
    row_count = SEQUENCE_BLOCKS * BLK
    complete_shape = (row_count, KEY_VALUE_HEADS, HEAD_SIZE)
    sampled_values = jnp.clip(jax.random.normal(jax.random.fold_in(key, 13), complete_shape, jnp.float32), -4.0, 4.0)
    return sampled_values.reshape(row_count, KEY_VALUE_HEADS * HEAD_SIZE).astype(jnp.bfloat16)


def draw_block_table(key, part):
    order = jax.random.permutation(jax.random.fold_in(key, 17), SEQUENCE_BLOCKS // 2).astype(jnp.int32)
    lower = order.reshape(N_CTX, BLK_DEV // 2)
    upper = SEQUENCE_BLOCKS - 1 - lower
    return jnp.concatenate([lower, upper], axis=1).astype(jnp.int32)


def draw_pattern(key, part):
    block_ids = jnp.arange(SEQUENCE_BLOCKS, dtype=jnp.int32)
    fixed_part = jnp.stack([block_ids, jnp.maximum(block_ids - 1, 0), jnp.zeros_like(block_ids)], axis=1)
    random_part = jax.random.randint(jax.random.fold_in(key, 19), (SEQUENCE_BLOCKS, KMAX - 3), 0, (block_ids + 1)[:, None], dtype=jnp.int32)
    return jnp.concatenate([fixed_part, random_part], axis=1).astype(jnp.int32)


def level_of(stream_key, shape, split, least, largest):
    loudness, own = 1.0, jax.random.fold_in(stream_key, 6)
    for dim, shards_of in split:
        draws = jnp.exp(jax.random.uniform(jax.random.fold_in(own, dim), (shards_of,), jnp.float32, least / len(split), largest / len(split)))
        loudness = loudness * jnp.repeat(draws, shape[dim] // shards_of).reshape([-1 if axis == dim else 1 for axis in range(len(shape))])
    return loudness


def scatter_about(rng, extent, deviation, most, pieces=(), kind=jnp.bfloat16):
    values = deviation * jax.random.normal(rng, extent, jnp.float32)
    if pieces:
        values = values * level_of(rng, extent, pieces, -0.22, 0.18)
    return jnp.clip(values, -most, most).astype(kind)


def setup_inputs(seed: int = 0, part: int = 0) -> dict:
    seeds = jax.random.split(jax.random.key(seed), 7)
    part_splits = jax.random.split(jax.random.fold_in(seeds[6], part), 7)
    return {
        "query_rows": draw_query_rows(jax.random.fold_in(jax.random.fold_in(seeds[6], part), 71), part),
        "key_rows": draw_key_rows(jax.random.fold_in(jax.random.fold_in(seeds[6], part), 71), part),
        "stored_value_rows": scatter_about(part_splits[2], (EPISODE_TOKENS, KEY_VALUE_HEADS * HEAD_SIZE), 1.0, 6.0, ((0, 4), (1, 2))),
        "out_grad": scatter_about(part_splits[3], (EPISODE_TOKENS, QUERY_HEADS * HEAD_SIZE), 1.0, 6.0, ((0, 4), (1, 2))),
        "block_table": draw_block_table(jax.random.fold_in(jax.random.fold_in(seeds[6], part), 71), part),
        "pattern": draw_pattern(jax.random.fold_in(jax.random.fold_in(seeds[6], part), 71), part),
    }


def slot_layout(block_table, pattern, held_seq):
    blocks = pattern.shape[0]
    slots = pattern.shape[1]
    block_ids = jnp.arange(blocks, dtype=jnp.int32)
    store_seq = block_table.reshape(-1)
    inverse = jnp.sum(jnp.where(store_seq[:, None] == block_ids[None, :], block_ids[:, None], 0), axis=0).astype(jnp.int32)
    onehot = (held_seq[:, None] == block_ids[None, :]).astype(jnp.int32)
    held_pattern = jnp.sum(onehot[:, :, None] * pattern[None, :, :], axis=1).astype(jnp.int32)
    key_store = jnp.sum(jnp.where(held_pattern[:, :, None] == block_ids[None, None, :], inverse[None, None, :], 0), axis=2).astype(jnp.int32)
    same = held_pattern[:, :, None] == held_pattern[:, None, :]
    slot_ids = jnp.arange(slots, dtype=jnp.int32)
    before = slot_ids[None, :] < slot_ids[:, None]
    live_slot = jnp.logical_not(jnp.any(same & before[None], axis=2))
    inner = jnp.arange(BLK, dtype=jnp.int32)
    query_pos = held_seq[:, None] * BLK + inner[None, :]
    key_pos = held_pattern[:, :, None] * BLK + inner[None, None, :]
    allowed = live_slot[:, None, :, None] & (key_pos[:, None, :, :] <= query_pos[:, :, None, None])
    return key_store, allowed


def attend_tiles(query_held, grad_held, key_tiles, value_tiles, allowed):
    scaling = HEAD_SIZE ** -0.5
    query_wide = query_held.astype(jnp.float32)
    grad_wide = grad_held.astype(jnp.float32)
    key_wide = key_tiles.astype(jnp.float32)
    value_wide = value_tiles.astype(jnp.float32)
    scores = jnp.einsum('biagd,bjkad->bagijk', query_wide, key_wide) * scaling
    scores = jnp.where(allowed[:, None, None], scores, -jnp.inf)
    row_max = jnp.max(scores, axis=(4, 5), keepdims=True)
    row_sum = jnp.sum(jnp.exp(scores - row_max), axis=(4, 5), keepdims=True)
    log_total = row_max + jnp.log(row_sum)
    prob_full = jnp.exp(scores - log_total)
    prob_low = prob_full.astype(jnp.bfloat16)
    attended_wide = jnp.einsum('bagijk,bjkad->biagd', prob_low.astype(jnp.float32), value_wide)
    attended = attended_wide.astype(jnp.bfloat16)
    row_dot = jnp.sum(grad_wide * attended_wide, axis=-1)
    row_dot = jnp.transpose(row_dot, (0, 2, 3, 1))[..., None, None]
    grad_prob = jnp.einsum('biagd,bjkad->bagijk', grad_wide, value_wide)
    grad_score = (prob_full * (grad_prob - row_dot) * scaling).astype(jnp.bfloat16)
    query_grad = jnp.einsum('bagijk,bjkad->biagd', grad_score.astype(jnp.float32), key_wide).astype(jnp.bfloat16)
    key_grads = jnp.einsum('bagijk,biagd->bjkad', grad_score.astype(jnp.float32), query_wide)
    value_grads = jnp.einsum('bagijk,biagd->bjkad', prob_low.astype(jnp.float32), grad_wide)
    return attended, query_grad, key_grads, value_grads


def reference(query_rows, key_rows, stored_value_rows, out_grad, block_table, pattern):
    blocks = pattern.shape[0]
    row_count = query_rows.shape[0]
    per_dev = block_table.shape[1]
    kv_heads = key_rows.shape[1] // HEAD_SIZE
    groups = query_rows.shape[1] // key_rows.shape[1]
    key_blocks = key_rows.reshape(blocks, BLK, kv_heads, HEAD_SIZE)
    value_blocks = stored_value_rows.reshape(blocks, BLK, kv_heads, HEAD_SIZE)

    def one_device(running, device):
        key_sums, value_sums = running
        held_seq = block_table[device]
        key_store, allowed = slot_layout(block_table, pattern, held_seq)
        first_row = (device * per_dev * BLK).astype(jnp.int32)
        query_held = lax.dynamic_slice_in_dim(query_rows, first_row, per_dev * BLK, 0).reshape(per_dev, BLK, kv_heads, groups, HEAD_SIZE)
        grad_held = lax.dynamic_slice_in_dim(out_grad, first_row, per_dev * BLK, 0).reshape(per_dev, BLK, kv_heads, groups, HEAD_SIZE)
        key_tiles = key_blocks[key_store]
        value_tiles = value_blocks[key_store]
        attended, query_grad, key_grads, value_grads = attend_tiles(query_held, grad_held, key_tiles, value_tiles, allowed)
        flat_slots = key_store.reshape(-1)
        key_partial = jnp.zeros((blocks, BLK, kv_heads, HEAD_SIZE), jnp.float32).at[flat_slots].add(key_grads.reshape(-1, BLK, kv_heads, HEAD_SIZE))
        value_partial = jnp.zeros((blocks, BLK, kv_heads, HEAD_SIZE), jnp.float32).at[flat_slots].add(value_grads.reshape(-1, BLK, kv_heads, HEAD_SIZE))
        key_low = lax.optimization_barrier(key_partial.astype(jnp.bfloat16))
        value_low = lax.optimization_barrier(value_partial.astype(jnp.bfloat16))
        key_sums = key_sums + key_low.astype(jnp.float32)
        value_sums = value_sums + value_low.astype(jnp.float32)
        return (key_sums, value_sums), (attended, query_grad)

    start = (jnp.zeros((blocks, BLK, kv_heads, HEAD_SIZE), jnp.float32), jnp.zeros((blocks, BLK, kv_heads, HEAD_SIZE), jnp.float32))
    (key_sums, value_sums), (attended, query_grad) = lax.scan(one_device, start, jnp.arange(N_CTX, dtype=jnp.int32))
    attended = attended.reshape(row_count, -1)
    query_grad = query_grad.reshape(row_count, -1)
    key_grad = key_sums.reshape(row_count, -1).astype(jnp.bfloat16)
    value_grad = value_sums.reshape(row_count, -1).astype(jnp.bfloat16)
    return (attended, query_grad, key_grad, value_grad)
```

```python
import functools

import jax
import jax.numpy as jnp
from jax import lax
from jax.experimental import pallas as pl
from jax.experimental.pallas import tpu as pltpu
from jax.sharding import PartitionSpec as P

HEAD_SIZE = 128
BLK = 128
MESH = pl.DeviceIdType.MESH
ROWS_CHUNK = 256
NEG = -1e30
SCALE = HEAD_SIZE ** (-0.5)
LOG2E = 1.4426950408889634


def slot_layout(block_table, pattern, held_seq):
    blocks = pattern.shape[0]
    slots = pattern.shape[1]
    block_ids = jnp.arange(blocks, dtype=jnp.int32)
    store_seq = block_table.reshape(-1)
    inverse = jnp.sum(
        jnp.where(store_seq[:, None] == block_ids[None, :], block_ids[:, None], 0), axis=0
    )
    onehot = (held_seq[:, None] == block_ids[None, :]).astype(jnp.int32)
    held_pattern = jnp.sum(onehot[:, :, None] * pattern[None, :, :], axis=1)
    key_store = jnp.sum(
        jnp.where(held_pattern[:, :, None] == block_ids[None, None, :], inverse[None, None, :], 0),
        axis=2,
    )
    same = held_pattern[:, :, None] == held_pattern[:, None, :]
    slot_ids = jnp.arange(slots, dtype=jnp.int32)
    before = slot_ids[None, :] < slot_ids[:, None]
    live_slot = jnp.logical_not(jnp.any(same & before[None], axis=2))
    inner = jnp.arange(BLK, dtype=jnp.int32)
    query_pos = held_seq[:, None] * BLK + inner[None, :]
    key_pos = held_pattern[:, :, None] * BLK + inner[None, None, :]
    allowed = live_slot[:, None, :, None] & (key_pos[:, None, :, :] <= query_pos[:, :, None, None])
    return (key_store, allowed)


def attend_tiles(query_held, grad_held, key_tiles, value_tiles, allowed):
    scaling = HEAD_SIZE ** (-0.5)
    scores = (
        jnp.einsum("biagd,bjkad->bagijk", query_held, key_tiles, preferred_element_type=jnp.float32)
        * scaling
    )
    scores = jnp.where(allowed[:, None, None], scores, -jnp.inf)
    row_max = jnp.max(scores, axis=(4, 5), keepdims=True)
    row_sum = jnp.sum(jnp.exp(scores - row_max), axis=(4, 5), keepdims=True)
    log_total = row_max + jnp.log(row_sum)
    prob_full = jnp.exp(scores - log_total)
    prob_low = prob_full.astype(jnp.bfloat16)
    attended_wide = jnp.einsum(
        "bagijk,bjkad->biagd", prob_low, value_tiles, preferred_element_type=jnp.float32
    )
    attended = attended_wide.astype(jnp.bfloat16)
    row_dot = jnp.sum(grad_held.astype(jnp.float32) * attended_wide, axis=-1)
    row_dot = jnp.transpose(row_dot, (0, 2, 3, 1))[..., None, None]
    grad_prob = jnp.einsum(
        "biagd,bjkad->bagijk", grad_held, value_tiles, preferred_element_type=jnp.float32
    )
    grad_score = (prob_full * (grad_prob - row_dot) * scaling).astype(jnp.bfloat16)
    query_grad = jnp.einsum(
        "bagijk,bjkad->biagd", grad_score, key_tiles, preferred_element_type=jnp.float32
    ).astype(jnp.bfloat16)
    key_grads = jnp.einsum(
        "bagijk,biagd->bjkad", grad_score, query_held, preferred_element_type=jnp.float32
    )
    value_grads = jnp.einsum(
        "bagijk,biagd->bjkad", prob_low, grad_held, preferred_element_type=jnp.float32
    )
    return (attended, query_grad, key_grads, value_grads)


def per_device_wide(query_rows, key_rows, stored_value_rows, out_grad, block_table, pattern):
    ctx_index = lax.axis_index("ctx")
    per_dev = block_table.shape[1]
    blocks = pattern.shape[0]
    kv_local = key_rows.shape[1] // HEAD_SIZE
    groups = query_rows.shape[1] // key_rows.shape[1]
    held_rows = per_dev * BLK
    held_seq = lax.dynamic_index_in_dim(block_table, ctx_index, 0, keepdims=False)
    key_store, allowed = slot_layout(block_table, pattern, held_seq)
    key_all, value_all = (
        lax.all_gather(key_rows, "ctx", axis=0, tiled=True),
        lax.all_gather(stored_value_rows, "ctx", axis=0, tiled=True),
    )
    key_blocks = key_all.reshape(blocks, BLK, kv_local, HEAD_SIZE)
    value_blocks = value_all.reshape(blocks, BLK, kv_local, HEAD_SIZE)
    key_tiles = key_blocks[key_store]
    value_tiles = value_blocks[key_store]
    query_held = query_rows.reshape(per_dev, BLK, kv_local, groups, HEAD_SIZE)
    grad_held = out_grad.reshape(per_dev, BLK, kv_local, groups, HEAD_SIZE)
    attended, query_grad, key_grads, value_grads = attend_tiles(
        query_held, grad_held, key_tiles, value_tiles, allowed
    )
    flat_slots = key_store.reshape(-1)

    def scattered(grads):
        partial = (
            jnp.zeros((blocks, BLK, kv_local, HEAD_SIZE), jnp.float32)
            .at[flat_slots]
            .add(grads.reshape(-1, BLK, kv_local, HEAD_SIZE))
        )
        return lax.psum_scatter(
            partial.reshape(blocks * BLK, -1).astype(jnp.bfloat16),
            "ctx",
            scatter_dimension=0,
            tiled=True,
        ).astype(jnp.bfloat16)

    return (
        attended.reshape(held_rows, -1),
        query_grad.reshape(held_rows, -1),
        scattered(key_grads),
        scattered(value_grads),
    )


def fused_kernel(
    heads, groups, blocks,
    bt_ref, pat_ref, q_hbm, k_hbm, v_hbm, g_hbm,
    att_hbm, dq_hbm, dk_hbm, dv_hbm,
    kv_all, kv_now, q_buf, g_buf, att_buf, dq_buf,
    qq, gg, qq_t, gg_t, key_slots, value_slots, prob, dscore, att_now, dq_now,
    d_slots, own_part, y_part, mate_send, mate_recv, y_send, y_recv, dkv_buf,
    load_sem, kv_sem, out_sem, dkv_sem, gather_send, gather_recv, red_send, red_recv,
):
    slots = blocks + 1
    half = blocks // 2
    width = groups * HEAD_SIZE
    rows = groups * BLK
    me = lax.axis_index("ctx")
    core, y = me % 2, me // 2
    mate = y * 2 + (1 - core)
    peer = (1 - y) * 2 + core
    cross = (1 - y) * 2 + (1 - core)

    kv_loads = []
    for h in range(heads):
        for i, ref in enumerate((k_hbm, v_hbm)):
            copy = pltpu.make_async_copy(
                ref.at[:, h * HEAD_SIZE : (h + 1) * HEAD_SIZE], kv_all.at[h, i, me], kv_sem.at[h, i]
            )
            copy.start()
            kv_loads.append(copy)
    loads = []
    for i, (src, dst) in enumerate(((q_hbm, q_buf), (g_hbm, g_buf))):
        for b in range(2):
            copy = pltpu.make_async_copy(
                src.at[b * BLK : (b + 1) * BLK], dst.at[b], load_sem.at[i, b]
            )
            copy.start()
            loads.append(copy)

    barrier = pltpu.get_barrier_semaphore()
    for other in (mate, peer):
        pl.semaphore_signal(barrier, inc=1, device_id={"ctx": other}, device_id_type=MESH)
    pl.semaphore_wait(barrier, 2)

    def gather_copy(h, source, target, kind):
        return pltpu.make_async_remote_copy(
            src_ref=kv_all.at[h, :, source],
            dst_ref=kv_all.at[h, :, source],
            send_sem=gather_send.at[h, kind],
            recv_sem=gather_recv.at[h, kind],
            device_id={"ctx": target},
            device_id_type=MESH,
        )

    def gather_arrival(h, source, kind):
        return gather_copy(h, source, mate, kind)

    def mate_copy(h):
        return pltpu.make_async_remote_copy(
            src_ref=mate_send.at[h],
            dst_ref=mate_recv.at[h],
            send_sem=red_send.at[h, 0],
            recv_sem=red_recv.at[h, 0],
            device_id={"ctx": mate},
            device_id_type=MESH,
        )

    def peer_copy(h):
        return pltpu.make_async_remote_copy(
            src_ref=y_send.at[h],
            dst_ref=y_recv.at[h],
            send_sem=red_send.at[h, 1],
            recv_sem=red_recv.at[h, 1],
            device_id={"ctx": peer},
            device_id_type=MESH,
        )

    def out_copy(h, b, i):
        buf, dst = ((att_buf, att_hbm), (dq_buf, dq_hbm))[i]
        return pltpu.make_async_copy(
            buf.at[h, b],
            dst.at[b * BLK : (b + 1) * BLK, pl.ds(pl.multiple_of(h * width, width), width)],
            out_sem.at[h, b, i],
        )

    for h in range(heads):
        kv_loads[2 * h].wait()
        kv_loads[2 * h + 1].wait()
        gather_copy(h, me, peer, 0).start()
        gather_copy(h, me, mate, 1).start()

    seq0, seq1 = bt_ref[me, 0], bt_ref[me, 1]
    lo, hi = jnp.minimum(seq0, seq1), jnp.maximum(seq0, seq1)
    at_lo = jnp.where(seq0 > seq1, 1, 0)
    at_hi = 1 - at_lo
    table = [bt_ref[g // 2, g % 2] for g in range(blocks)]
    homes, biases, is_lo = [], [], []
    for p in range(slots):
        if p == 0:
            mine, key_seq, query_seq = None, lo, lo
        elif p >= half:
            mine, key_seq, query_seq = None, p - lo - 1, hi
        else:
            mine = p <= lo
            key_seq = jnp.where(mine, lo - p, p - lo - 1)
            query_seq = jnp.where(mine, lo, hi)
        home = jnp.int32(0)
        for g in range(blocks):
            home = jnp.where(table[g] == key_seq, g, home)
        homes.append(home)
        is_lo.append(mine)
        if p in (0, slots - 1):
            biases.append(None)
        else:
            hits = jnp.int32(0)
            for j in range(pat_ref.shape[1]):
                hits = hits + jnp.where(pat_ref[query_seq, j] == key_seq, 1, 0)
            biases.append(jnp.where(hits > 0, jnp.float32(0), jnp.float32(NEG)))
    in_lo = [None if m is None else jnp.where(m, jnp.float32(1), jnp.float32(0)) for m in is_lo]

    zeros = jnp.zeros((BLK, HEAD_SIZE), jnp.bfloat16)
    for ref in (key_slots, value_slots):
        for p in range(slots):
            if p == 0:
                ref[p * BLK : (p + 1) * BLK, HEAD_SIZE:] = zeros
            elif p >= half:
                ref[p * BLK : (p + 1) * BLK, :HEAD_SIZE] = zeros

    for copy in loads:
        copy.wait()

    def forward(h):
        gather_arrival(h, peer, 0).wait_recv()
        gather_copy(h, peer, mate, 2).start()

    def second_stage(h):
        mate_copy(h).wait_recv()
        for i in range(2):
            y_send[h, i] = (y_part[h, i] + mate_recv[h, 1, i].astype(jnp.float32)).astype(
                jnp.bfloat16
            )
        peer_copy(h).start()

    forward(0)

    def one_head(h, carry):
        first = pl.multiple_of(h * width, width)
        for src, dst, dst_t in ((q_buf, qq, qq_t), (g_buf, gg, gg_t)):
            for g in range(groups):
                cols = pl.ds(pl.multiple_of(first + g * HEAD_SIZE, HEAD_SIZE), HEAD_SIZE)
                for part, at in ((0, at_lo), (1, at_hi)):
                    tile = src[at, :, cols]
                    dst[g * BLK : (g + 1) * BLK, part * HEAD_SIZE : (part + 1) * HEAD_SIZE] = tile
                    dst_t[part * HEAD_SIZE : (part + 1) * HEAD_SIZE, g * BLK : (g + 1) * BLK] = tile.T

        gather_arrival(h, mate, 1).wait_recv()
        gather_arrival(h, cross, 2).wait_recv()
        for i in range(2):
            for c in range(blocks // 2):
                for b in range(2):
                    kv_now[i, c * 2 + b] = kv_all[h, i, c, b * BLK : (b + 1) * BLK]
        for i, ref in enumerate((key_slots, value_slots)):
            for p in range(slots):
                tile = kv_now[i, homes[p]]
                at = slice(p * BLK, (p + 1) * BLK)
                if p == 0:
                    ref[at, :HEAD_SIZE] = tile
                elif p >= half:
                    ref[at, HEAD_SIZE:] = tile
                else:
                    wide = tile.astype(jnp.float32)
                    ref[at, :HEAD_SIZE] = (wide * in_lo[p]).astype(jnp.bfloat16)
                    ref[at, HEAD_SIZE:] = (wide * (1.0 - in_lo[p])).astype(jnp.bfloat16)

        def one_chunk(c, carry):
            at = pl.ds(pl.multiple_of(c * ROWS_CHUNK, ROWS_CHUNK), ROWS_CHUNK)
            nt = (((1,), (1,)), ((), ()))
            score = lax.dot_general(
                qq[at, :], key_slots[...], nt, preferred_element_type=jnp.float32
            )
            row = lax.broadcasted_iota(jnp.int32, (ROWS_CHUNK, BLK), 0) % BLK
            col = lax.broadcasted_iota(jnp.int32, (ROWS_CHUNK, BLK), 1)
            causal = col <= row
            tiles = []
            for p in range(slots):
                tile = score[:, p * BLK : (p + 1) * BLK]
                tiles.append(
                    jnp.where(causal, tile, NEG) if biases[p] is None else tile + biases[p]
                )
            max_lo, max_hi = tiles[0], tiles[half]
            for p in range(1, slots):
                if p < half:
                    max_lo = jnp.maximum(max_lo, tiles[p] + (1.0 - in_lo[p]) * NEG)
                    max_hi = jnp.maximum(max_hi, tiles[p] + in_lo[p] * NEG)
                elif p > half:
                    max_hi = jnp.maximum(max_hi, tiles[p])
            max_lo = jnp.max(max_lo, axis=1, keepdims=True)
            max_hi = jnp.max(max_hi, axis=1, keepdims=True)

            def pick(p, of_lo, of_hi):
                if p == 0:
                    return of_lo
                if p >= half:
                    return of_hi
                return of_lo * in_lo[p] + of_hi * (1.0 - in_lo[p])

            sum_lo = sum_hi = None
            for p in range(slots):
                tiles[p] = jnp.exp2((tiles[p] - pick(p, max_lo, max_hi)) * (SCALE * LOG2E))
                if p == 0:
                    sum_lo = tiles[p]
                elif p < half:
                    sum_lo = sum_lo + tiles[p] * in_lo[p]
                    part = tiles[p] * (1.0 - in_lo[p])
                    sum_hi = part if sum_hi is None else sum_hi + part
                else:
                    sum_hi = tiles[p] if sum_hi is None else sum_hi + tiles[p]
            inv_lo = 1.0 / jnp.sum(sum_lo, axis=1, keepdims=True)
            inv_hi = 1.0 / jnp.sum(sum_hi, axis=1, keepdims=True)
            for p in range(slots):
                tiles[p] = tiles[p] * pick(p, inv_lo, inv_hi)
                prob[at, p * BLK : (p + 1) * BLK] = tiles[p].astype(jnp.bfloat16)
            wide = jnp.dot(prob[at, :], value_slots[...], preferred_element_type=jnp.float32)
            att_now[0, at, :] = wide[:, :HEAD_SIZE].astype(jnp.bfloat16)
            att_now[1, at, :] = wide[:, HEAD_SIZE:].astype(jnp.bfloat16)
            dots = wide * gg[at, :].astype(jnp.float32)
            dot_lo = jnp.sum(dots[:, :HEAD_SIZE], axis=1, keepdims=True)
            dot_hi = jnp.sum(dots[:, HEAD_SIZE:], axis=1, keepdims=True)
            dprob = lax.dot_general(
                gg[at, :], value_slots[...], nt, preferred_element_type=jnp.float32
            )
            for p in range(slots):
                cols = slice(p * BLK, (p + 1) * BLK)
                dscore[at, cols] = (tiles[p] * (dprob[:, cols] - pick(p, dot_lo, dot_hi))).astype(
                    jnp.bfloat16
                )
            dq = SCALE * jnp.dot(dscore[at, :], key_slots[...], preferred_element_type=jnp.float32)
            dq_now[0, at, :] = dq[:, :HEAD_SIZE].astype(jnp.bfloat16)
            dq_now[1, at, :] = dq[:, HEAD_SIZE:].astype(jnp.bfloat16)
            return carry

        lax.fori_loop(0, rows // ROWS_CHUNK, one_chunk, 0)

        @pl.when(h < heads - 1)
        def _():
            forward(h + 1)

        @pl.when(h > 0)
        def _():
            second_stage(h - 1)

        for b in range(2):
            from_now = jnp.where(at_lo == b, 0, 1)
            for g in range(groups):
                cols = slice(g * HEAD_SIZE, (g + 1) * HEAD_SIZE)
                att_buf[h, b, :, cols] = att_now[from_now, g * BLK : (g + 1) * BLK, :]
                dq_buf[h, b, :, cols] = dq_now[from_now, g * BLK : (g + 1) * BLK, :]
            out_copy(h, b, 0).start()
            out_copy(h, b, 1).start()

        for i, (left, right) in enumerate(((qq_t, dscore), (gg_t, prob))):
            grads = jnp.dot(left[...], right[...], preferred_element_type=jnp.float32)
            for p in range(slots):
                cols = slice(p * BLK, (p + 1) * BLK)
                if p == 0:
                    d_slots[i, p] = grads[:HEAD_SIZE, cols]
                elif p >= half:
                    d_slots[i, p] = grads[HEAD_SIZE:, cols]
                else:
                    d_slots[i, p] = grads[:HEAD_SIZE, cols] * in_lo[p] + grads[
                        HEAD_SIZE:, cols
                    ] * (1.0 - in_lo[p])

        def partial(i, target, b):
            seq = bt_ref[target, b]
            slot_lo = jnp.maximum(lo - seq, 0)
            slot_hi = jnp.minimum(lo + 1 + seq, slots - 1)
            scale = SCALE if i == 0 else 1.0
            of_lo = jnp.where(seq <= lo, jnp.float32(scale), jnp.float32(0))
            of_hi = jnp.where(seq <= hi, jnp.float32(scale), jnp.float32(0))
            return (d_slots[i, slot_lo] * of_lo + d_slots[i, slot_hi] * of_hi).T

        for i in range(2):
            for b in range(2):
                at = slice(b * BLK, (b + 1) * BLK)
                mate_send[h, 0, i, at] = partial(i, mate, b).astype(jnp.bfloat16)
                mate_send[h, 1, i, at] = partial(i, cross, b).astype(jnp.bfloat16)
        mate_copy(h).start()
        for i in range(2):
            for b in range(2):
                at = slice(b * BLK, (b + 1) * BLK)
                y_part[h, i, at] = partial(i, peer, b)
                own_part[h, i, at] = partial(i, me, b)
        return carry

    lax.fori_loop(0, heads, one_head, 0)
    second_stage(heads - 1)

    dkv_copies = []
    for h in range(heads):
        peer_copy(h).wait_recv()
        for i, dst in enumerate((dk_hbm, dv_hbm)):
            total = (
                own_part[h, i]
                + mate_recv[h, 0, i].astype(jnp.float32)
                + y_recv[h, i].astype(jnp.float32)
            )
            dkv_buf[h, i] = total.astype(jnp.bfloat16)
            copy = pltpu.make_async_copy(
                dkv_buf.at[h, i], dst.at[:, h * HEAD_SIZE : (h + 1) * HEAD_SIZE], dkv_sem.at[h, i]
            )
            copy.start()
            dkv_copies.append(copy)

    for h in range(heads):
        gather_copy(h, me, peer, 0).wait_send()
        gather_copy(h, me, mate, 1).wait_send()
        gather_copy(h, peer, mate, 2).wait_send()
        mate_copy(h).wait_send()
        peer_copy(h).wait_send()
        for b in range(2):
            out_copy(h, b, 0).wait()
            out_copy(h, b, 1).wait()
    for copy in dkv_copies:
        copy.wait()


def per_device_fused(query_rows, key_rows, stored_value_rows, out_grad, block_table, pattern):
    blocks = pattern.shape[0]
    held, kv_width = key_rows.shape
    heads = kv_width // HEAD_SIZE
    groups = query_rows.shape[1] // kv_width
    width = groups * HEAD_SIZE
    rows = groups * BLK
    slots = blocks + 1
    bf16, f32 = jnp.bfloat16, jnp.float32
    vmem, dma = pltpu.VMEM, pltpu.SemaphoreType.DMA
    ctx = blocks // 2
    pair = 2 * HEAD_SIZE
    scratch = [
        vmem((heads, 2, ctx, held, HEAD_SIZE), bf16),
        vmem((2, blocks, BLK, HEAD_SIZE), bf16),
        vmem((2, BLK, heads * width), bf16),
        vmem((2, BLK, heads * width), bf16),
        vmem((heads, 2, BLK, width), bf16),
        vmem((heads, 2, BLK, width), bf16),
        vmem((rows, pair), bf16),
        vmem((rows, pair), bf16),
        vmem((pair, rows), bf16),
        vmem((pair, rows), bf16),
        vmem((slots * BLK, pair), bf16),
        vmem((slots * BLK, pair), bf16),
        vmem((rows, slots * BLK), bf16),
        vmem((rows, slots * BLK), bf16),
        vmem((2, rows, HEAD_SIZE), bf16),
        vmem((2, rows, HEAD_SIZE), bf16),
        vmem((2, slots, HEAD_SIZE, BLK), f32),
        vmem((heads, 2, held, HEAD_SIZE), f32),
        vmem((heads, 2, held, HEAD_SIZE), f32),
        vmem((heads, 2, 2, held, HEAD_SIZE), bf16),
        vmem((heads, 2, 2, held, HEAD_SIZE), bf16),
        vmem((heads, 2, held, HEAD_SIZE), bf16),
        vmem((heads, 2, held, HEAD_SIZE), bf16),
        vmem((heads, 2, held, HEAD_SIZE), bf16),
        dma((2, 2)),
        dma((heads, 2)),
        dma((heads, 2, 2)),
        dma((heads, 2)),
        dma((heads, 3)),
        dma((heads, 3)),
        dma((heads, 2)),
        dma((heads, 2)),
    ]
    smem = pl.BlockSpec(memory_space=pltpu.SMEM)
    hbm = pl.BlockSpec(memory_space=pl.ANY)
    return pl.pallas_call(
        functools.partial(fused_kernel, heads, groups, blocks),
        out_shape=(
            jax.ShapeDtypeStruct(query_rows.shape, bf16),
            jax.ShapeDtypeStruct(query_rows.shape, bf16),
            jax.ShapeDtypeStruct(key_rows.shape, bf16),
            jax.ShapeDtypeStruct(key_rows.shape, bf16),
        ),
        in_specs=[smem, smem, hbm, hbm, hbm, hbm],
        out_specs=(hbm, hbm, hbm, hbm),
        scratch_shapes=scratch,
        compiler_params=pltpu.CompilerParams(
            collective_id=0, has_side_effects=True, vmem_limit_bytes=52 * 1024 * 1024
        ),
        cost_estimate=pl.CostEstimate(
            flops=12 * heads * rows * pair * slots * BLK,
            bytes_accessed=8 * query_rows.size + 8 * key_rows.size,
            transcendentals=heads * rows * slots * BLK,
        ),
    )(block_table, pattern, query_rows, key_rows, stored_value_rows, out_grad)


def solution(mesh):
    row_spec = P(("dp", "ctx"), "head")
    in_specs = (row_spec, row_spec, row_spec, row_spec, P("dp", None), P("dp", None))
    out_specs = (row_spec, row_spec, row_spec, row_spec)

    def per_device(query_rows, key_rows, stored_value_rows, out_grad, block_table, pattern):
        fits = mesh.shape["ctx"] == 4 and block_table.shape == (4, 2)
        body = per_device_fused if fits else per_device_wide
        return body(query_rows, key_rows, stored_value_rows, out_grad, block_table, pattern)

    return jax.shard_map(
        per_device, mesh=mesh, in_specs=in_specs, out_specs=out_specs, check_vma=False
    )
```

```python
import functools

import jax
import jax.numpy as jnp
from jax import lax
from jax.experimental import pallas as pl
from jax.experimental.pallas import tpu as pltpu
from jax.sharding import PartitionSpec as P

HEAD_SIZE = 128
BLK = 128
MESH = pl.DeviceIdType.MESH
ROWS_CHUNK = 256
SUB = 32
NEG = -1e30
SCALE = HEAD_SIZE ** (-0.5)
LOG2E = 1.4426950408889634


def slot_layout(block_table, pattern, held_seq):
    blocks = pattern.shape[0]
    slots = pattern.shape[1]
    block_ids = jnp.arange(blocks, dtype=jnp.int32)
    store_seq = block_table.reshape(-1)
    inverse = jnp.sum(
        jnp.where(store_seq[:, None] == block_ids[None, :], block_ids[:, None], 0), axis=0
    )
    onehot = (held_seq[:, None] == block_ids[None, :]).astype(jnp.int32)
    held_pattern = jnp.sum(onehot[:, :, None] * pattern[None, :, :], axis=1)
    key_store = jnp.sum(
        jnp.where(held_pattern[:, :, None] == block_ids[None, None, :], inverse[None, None, :], 0),
        axis=2,
    )
    same = held_pattern[:, :, None] == held_pattern[:, None, :]
    slot_ids = jnp.arange(slots, dtype=jnp.int32)
    before = slot_ids[None, :] < slot_ids[:, None]
    live_slot = jnp.logical_not(jnp.any(same & before[None], axis=2))
    inner = jnp.arange(BLK, dtype=jnp.int32)
    query_pos = held_seq[:, None] * BLK + inner[None, :]
    key_pos = held_pattern[:, :, None] * BLK + inner[None, None, :]
    allowed = live_slot[:, None, :, None] & (key_pos[:, None, :, :] <= query_pos[:, :, None, None])
    return (key_store, allowed)


def attend_tiles(query_held, grad_held, key_tiles, value_tiles, allowed):
    scaling = HEAD_SIZE ** (-0.5)
    scores = (
        jnp.einsum("biagd,bjkad->bagijk", query_held, key_tiles, preferred_element_type=jnp.float32)
        * scaling
    )
    scores = jnp.where(allowed[:, None, None], scores, -jnp.inf)
    row_max = jnp.max(scores, axis=(4, 5), keepdims=True)
    row_sum = jnp.sum(jnp.exp(scores - row_max), axis=(4, 5), keepdims=True)
    log_total = row_max + jnp.log(row_sum)
    prob_full = jnp.exp(scores - log_total)
    prob_low = prob_full.astype(jnp.bfloat16)
    attended_wide = jnp.einsum(
        "bagijk,bjkad->biagd", prob_low, value_tiles, preferred_element_type=jnp.float32
    )
    attended = attended_wide.astype(jnp.bfloat16)
    row_dot = jnp.sum(grad_held.astype(jnp.float32) * attended_wide, axis=-1)
    row_dot = jnp.transpose(row_dot, (0, 2, 3, 1))[..., None, None]
    grad_prob = jnp.einsum(
        "biagd,bjkad->bagijk", grad_held, value_tiles, preferred_element_type=jnp.float32
    )
    grad_score = (prob_full * (grad_prob - row_dot) * scaling).astype(jnp.bfloat16)
    query_grad = jnp.einsum(
        "bagijk,bjkad->biagd", grad_score, key_tiles, preferred_element_type=jnp.float32
    ).astype(jnp.bfloat16)
    key_grads = jnp.einsum(
        "bagijk,biagd->bjkad", grad_score, query_held, preferred_element_type=jnp.float32
    )
    value_grads = jnp.einsum(
        "bagijk,biagd->bjkad", prob_low, grad_held, preferred_element_type=jnp.float32
    )
    return (attended, query_grad, key_grads, value_grads)


def per_device_wide(query_rows, key_rows, stored_value_rows, out_grad, block_table, pattern):
    ctx_index = lax.axis_index("ctx")
    per_dev = block_table.shape[1]
    blocks = pattern.shape[0]
    kv_local = key_rows.shape[1] // HEAD_SIZE
    groups = query_rows.shape[1] // key_rows.shape[1]
    held_rows = per_dev * BLK
    held_seq = lax.dynamic_index_in_dim(block_table, ctx_index, 0, keepdims=False)
    key_store, allowed = slot_layout(block_table, pattern, held_seq)
    key_all, value_all = (
        lax.all_gather(key_rows, "ctx", axis=0, tiled=True),
        lax.all_gather(stored_value_rows, "ctx", axis=0, tiled=True),
    )
    key_blocks = key_all.reshape(blocks, BLK, kv_local, HEAD_SIZE)
    value_blocks = value_all.reshape(blocks, BLK, kv_local, HEAD_SIZE)
    key_tiles = key_blocks[key_store]
    value_tiles = value_blocks[key_store]
    query_held = query_rows.reshape(per_dev, BLK, kv_local, groups, HEAD_SIZE)
    grad_held = out_grad.reshape(per_dev, BLK, kv_local, groups, HEAD_SIZE)
    attended, query_grad, key_grads, value_grads = attend_tiles(
        query_held, grad_held, key_tiles, value_tiles, allowed
    )
    flat_slots = key_store.reshape(-1)

    def scattered(grads):
        partial = (
            jnp.zeros((blocks, BLK, kv_local, HEAD_SIZE), jnp.float32)
            .at[flat_slots]
            .add(grads.reshape(-1, BLK, kv_local, HEAD_SIZE))
        )
        return lax.psum_scatter(
            partial.reshape(blocks * BLK, -1).astype(jnp.bfloat16),
            "ctx",
            scatter_dimension=0,
            tiled=True,
        ).astype(jnp.bfloat16)

    return (
        attended.reshape(held_rows, -1),
        query_grad.reshape(held_rows, -1),
        scattered(key_grads),
        scattered(value_grads),
    )


def fused_kernel(
    heads, groups, blocks,
    bt_ref, pat_ref, q_hbm, k_hbm, v_hbm, g_hbm,
    att_hbm, dq_hbm, dk_hbm, dv_hbm,
    kv_all, kv_now, q_buf, g_buf, att_buf, dq_buf,
    qq, gg, qq_t, gg_t, q_scaled, g_scaled, key_slots, value_slots, key_t, value_t, s_buf, d_buf, prob, dscore, att_now, dq_now,
    d_slots, own_part, y_part, mate_send, mate_recv, y_send, y_recv, dkv_buf,
    load_sem, kv_sem, out_sem, dkv_sem, gather_send, gather_recv, red_send, red_recv,
):
    slots = blocks + 1
    half = blocks // 2
    width = groups * HEAD_SIZE
    rows = groups * BLK
    me = lax.axis_index("ctx")
    core, y = me % 2, me // 2
    mate = y * 2 + (1 - core)
    peer = (1 - y) * 2 + core
    cross = (1 - y) * 2 + (1 - core)

    kv_loads = []
    for h in range(heads):
        for i, ref in enumerate((k_hbm, v_hbm)):
            copy = pltpu.make_async_copy(
                ref.at[:, h * HEAD_SIZE : (h + 1) * HEAD_SIZE], kv_all.at[h, i, me], kv_sem.at[h, i]
            )
            copy.start()
            kv_loads.append(copy)
    loads = []
    for i, (src, dst) in enumerate(((q_hbm, q_buf), (g_hbm, g_buf))):
        for b in range(2):
            copy = pltpu.make_async_copy(
                src.at[b * BLK : (b + 1) * BLK], dst.at[b], load_sem.at[i, b]
            )
            copy.start()
            loads.append(copy)

    barrier = pltpu.get_barrier_semaphore()
    for other in (mate, peer):
        pl.semaphore_signal(barrier, inc=1, device_id={"ctx": other}, device_id_type=MESH)
    pl.semaphore_wait(barrier, 2)

    def gather_copy(h, source, target, kind):
        return pltpu.make_async_remote_copy(
            src_ref=kv_all.at[h, :, source],
            dst_ref=kv_all.at[h, :, source],
            send_sem=gather_send.at[h, kind],
            recv_sem=gather_recv.at[h, kind],
            device_id={"ctx": target},
            device_id_type=MESH,
        )

    def gather_arrival(h, source, kind):
        return gather_copy(h, source, mate, kind)

    def mate_copy(h, i):
        return pltpu.make_async_remote_copy(
            src_ref=mate_send.at[h, i],
            dst_ref=mate_recv.at[h, i],
            send_sem=red_send.at[h, 0, i],
            recv_sem=red_recv.at[h, 0, i],
            device_id={"ctx": mate},
            device_id_type=MESH,
        )

    def peer_copy(h, i):
        return pltpu.make_async_remote_copy(
            src_ref=y_send.at[h, i],
            dst_ref=y_recv.at[h, i],
            send_sem=red_send.at[h, 1, i],
            recv_sem=red_recv.at[h, 1, i],
            device_id={"ctx": peer},
            device_id_type=MESH,
        )

    def out_copy(h, b, i):
        buf, dst = ((att_buf, att_hbm), (dq_buf, dq_hbm))[i]
        return pltpu.make_async_copy(
            buf.at[h, b],
            dst.at[b * BLK : (b + 1) * BLK, pl.ds(pl.multiple_of(h * width, width), width)],
            out_sem.at[h, b, i],
        )

    for h in range(heads):
        kv_loads[2 * h].wait()
        kv_loads[2 * h + 1].wait()
        gather_copy(h, me, peer, 0).start()
        gather_copy(h, me, mate, 1).start()

    seq0, seq1 = bt_ref[me, 0], bt_ref[me, 1]
    lo, hi = jnp.minimum(seq0, seq1), jnp.maximum(seq0, seq1)
    at_lo = jnp.where(seq0 > seq1, 1, 0)
    at_hi = 1 - at_lo
    table = [bt_ref[g // 2, g % 2] for g in range(blocks)]
    homes, biases, is_lo = [], [], []
    for p in range(slots):
        if p == 0:
            mine, key_seq, query_seq = None, lo, lo
        elif p >= half:
            mine, key_seq, query_seq = None, p - lo - 1, hi
        else:
            mine = p <= lo
            key_seq = jnp.where(mine, lo - p, p - lo - 1)
            query_seq = jnp.where(mine, lo, hi)
        home = jnp.int32(0)
        for g in range(blocks):
            home = jnp.where(table[g] == key_seq, g, home)
        homes.append(home)
        is_lo.append(mine)
        if p in (0, slots - 1):
            biases.append(None)
        else:
            hits = jnp.int32(0)
            for j in range(pat_ref.shape[1]):
                hits = hits + jnp.where(pat_ref[query_seq, j] == key_seq, 1, 0)
            biases.append(jnp.where(hits > 0, jnp.float32(0), jnp.float32(NEG)))
    bias_lo = [None if m is None else jnp.where(m, x, NEG) for m, x in zip(is_lo, biases)]
    bias_hi = [None if m is None else jnp.where(m, NEG, x) for m, x in zip(is_lo, biases)]
    in_lo = [None if m is None else jnp.where(m, jnp.float32(1), jnp.float32(0)) for m in is_lo]

    zeros = jnp.zeros((BLK, HEAD_SIZE), jnp.bfloat16)
    for ref, ref_t in ((key_slots, key_t), (value_slots, value_t)):
        for p in range(slots):
            at = slice(p * BLK, (p + 1) * BLK)
            if p == 0:
                ref[at, HEAD_SIZE:] = zeros
                ref_t[HEAD_SIZE:, at] = zeros
            elif p >= half:
                ref[at, :HEAD_SIZE] = zeros
                ref_t[:HEAD_SIZE, at] = zeros

    for copy in loads:
        copy.wait()

    def forward(h):
        gather_arrival(h, peer, 0).wait_recv()
        gather_copy(h, peer, mate, 2).start()

    def second_stage(h, i):
        mate_copy(h, i).wait_recv()
        y_send[h, i] = (y_part[h, i] + mate_recv[h, i, 1].astype(jnp.float32)).astype(jnp.bfloat16)
        peer_copy(h, i).start()

    forward(0)

    def one_head(h, carry):
        first = pl.multiple_of(h * width, width)
        for src, dst in ((q_buf, qq), (g_buf, gg)):
            for g in range(groups):
                cols = pl.ds(pl.multiple_of(first + g * HEAD_SIZE, HEAD_SIZE), HEAD_SIZE)
                for part, at in ((0, at_lo), (1, at_hi)):
                    tile = src[at, :, cols]
                    dst[g * BLK : (g + 1) * BLK, part * HEAD_SIZE : (part + 1) * HEAD_SIZE] = tile

        gather_arrival(h, mate, 1).wait_recv()
        gather_arrival(h, cross, 2).wait_recv()
        for i in range(2):
            for c in range(blocks // 2):
                for b in range(2):
                    kv_now[i, c * 2 + b] = kv_all[h, i, c, b * BLK : (b + 1) * BLK]
        for i, (ref, ref_t) in enumerate(((key_slots, key_t), (value_slots, value_t))):
            for p in range(slots):
                tile = kv_now[i, homes[p]]
                tile_t = tile.T
                at = slice(p * BLK, (p + 1) * BLK)
                if p == 0:
                    ref[at, :HEAD_SIZE] = tile
                    ref_t[:HEAD_SIZE, at] = tile_t
                elif p >= half:
                    ref[at, HEAD_SIZE:] = tile
                    ref_t[HEAD_SIZE:, at] = tile_t
                else:
                    for target, index, value in (
                        (ref, (at, slice(0, HEAD_SIZE)), tile),
                        (ref_t, (slice(0, HEAD_SIZE), at), tile_t),
                    ):
                        wide = value.astype(jnp.float32)
                        target[index] = (wide * in_lo[p]).astype(jnp.bfloat16)
                    for target, index, value in (
                        (ref, (at, slice(HEAD_SIZE, None)), tile),
                        (ref_t, (slice(HEAD_SIZE, None), at), tile_t),
                    ):
                        wide = value.astype(jnp.float32)
                        target[index] = (wide * (1.0 - in_lo[p])).astype(jnp.bfloat16)

        def matmuls(c):
            at = slice(c * ROWS_CHUNK, (c + 1) * ROWS_CHUNK)
            s_buf[c % 2] = jnp.dot(qq[at, :], key_t[...], preferred_element_type=jnp.float32)
            d_buf[c % 2] = jnp.dot(gg[at, :], value_t[...], preferred_element_type=jnp.float32)

        def pick(p, of_lo, of_hi):
            if p == 0:
                return of_lo
            if p >= half:
                return of_hi
            return jnp.where(is_lo[p], of_lo, of_hi)

        def softmax(c, r):
            rows_at = slice(c * ROWS_CHUNK + r, c * ROWS_CHUNK + r + SUB)
            inner = slice(r, r + SUB)
            row = lax.broadcasted_iota(jnp.int32, (SUB, BLK), 0) + (c * ROWS_CHUNK + r) % BLK
            col = lax.broadcasted_iota(jnp.int32, (SUB, BLK), 1)
            tiles = [s_buf[c % 2, inner, p * BLK : (p + 1) * BLK] for p in range(slots)]
            for p in (0, slots - 1):
                tiles[p] = jnp.where(col <= row, tiles[p], NEG)
            max_lo, max_hi = tiles[0], tiles[slots - 1]
            for p in range(1, slots - 1):
                if p < half:
                    max_lo = jnp.maximum(max_lo, tiles[p] + bias_lo[p])
                    max_hi = jnp.maximum(max_hi, tiles[p] + bias_hi[p])
                else:
                    max_hi = jnp.maximum(max_hi, tiles[p] + biases[p])
            max_lo = jnp.max(max_lo, axis=1, keepdims=True)
            max_hi = jnp.max(max_hi, axis=1, keepdims=True)
            sum_lo = sum_hi = None
            for p in range(slots):
                top = pick(p, max_lo, max_hi)
                if biases[p] is not None:
                    top = top - biases[p]
                tile = jnp.exp2((tiles[p] - top) * (SCALE * LOG2E))
                s_buf[c % 2, inner, p * BLK : (p + 1) * BLK] = tile
                prob[rows_at, p * BLK : (p + 1) * BLK] = tile.astype(jnp.bfloat16)
                if p == 0:
                    sum_lo = tile
                elif p < half:
                    sum_lo = sum_lo + jnp.where(is_lo[p], tile, 0.0)
                    part = jnp.where(is_lo[p], 0.0, tile)
                    sum_hi = part if sum_hi is None else sum_hi + part
                else:
                    sum_hi = tile if sum_hi is None else sum_hi + tile
            inv_lo = 1.0 / jnp.sum(sum_lo, axis=1, keepdims=True)
            inv_hi = 1.0 / jnp.sum(sum_hi, axis=1, keepdims=True)
            for src, dst in ((qq, q_scaled), (gg, g_scaled)):
                for cols, inv in ((slice(0, HEAD_SIZE), inv_lo), (slice(HEAD_SIZE, None), inv_hi)):
                    dst[inner, cols] = (src[rows_at, cols].astype(jnp.float32) * inv).astype(
                        jnp.bfloat16
                    )
            return inv_lo, inv_hi

        def finish(c):
            at = slice(c * ROWS_CHUNK, (c + 1) * ROWS_CHUNK)
            inverses = [softmax(c, r) for r in range(0, ROWS_CHUNK, SUB)]
            wide = jnp.dot(prob[at, :], value_slots[...], preferred_element_type=jnp.float32)
            for src, dst in ((q_scaled, qq_t), (g_scaled, gg_t)):
                dst[:, at] = src[...].T
            for n, (inv_lo, inv_hi) in enumerate(inverses):
                inner = slice(n * SUB, (n + 1) * SUB)
                rows_at = slice(c * ROWS_CHUNK + n * SUB, c * ROWS_CHUNK + (n + 1) * SUB)
                of_lo = wide[inner, :HEAD_SIZE] * inv_lo
                of_hi = wide[inner, HEAD_SIZE:] * inv_hi
                att_now[0, rows_at, :] = of_lo.astype(jnp.bfloat16)
                att_now[1, rows_at, :] = of_hi.astype(jnp.bfloat16)
                grad = gg[rows_at, :].astype(jnp.float32)
                dot_lo = jnp.sum(of_lo * grad[:, :HEAD_SIZE], axis=1, keepdims=True)
                dot_hi = jnp.sum(of_hi * grad[:, HEAD_SIZE:], axis=1, keepdims=True)
                for p in range(slots):
                    cols = slice(p * BLK, (p + 1) * BLK)
                    dscore[rows_at, cols] = (
                        s_buf[c % 2, inner, cols]
                        * (d_buf[c % 2, inner, cols] - pick(p, dot_lo, dot_hi))
                    ).astype(jnp.bfloat16)
            dq = jnp.dot(dscore[at, :], key_slots[...], preferred_element_type=jnp.float32)
            for n, (inv_lo, inv_hi) in enumerate(inverses):
                inner = slice(n * SUB, (n + 1) * SUB)
                rows_at = slice(c * ROWS_CHUNK + n * SUB, c * ROWS_CHUNK + (n + 1) * SUB)
                dq_now[0, rows_at, :] = (dq[inner, :HEAD_SIZE] * (inv_lo * SCALE)).astype(
                    jnp.bfloat16
                )
                dq_now[1, rows_at, :] = (dq[inner, HEAD_SIZE:] * (inv_hi * SCALE)).astype(
                    jnp.bfloat16
                )

        matmuls(0)
        for c in range(rows // ROWS_CHUNK):
            if c + 1 < rows // ROWS_CHUNK:
                matmuls(c + 1)
            finish(c)

        @pl.when(h < heads - 1)
        def _():
            forward(h + 1)

        @pl.when(h > 0)
        def _():
            second_stage(h - 1, 0)

        for b in range(2):
            from_now = jnp.where(at_lo == b, 0, 1)
            for g in range(groups):
                cols = slice(g * HEAD_SIZE, (g + 1) * HEAD_SIZE)
                att_buf[h, b, :, cols] = att_now[from_now, g * BLK : (g + 1) * BLK, :]
                dq_buf[h, b, :, cols] = dq_now[from_now, g * BLK : (g + 1) * BLK, :]
            out_copy(h, b, 0).start()
            out_copy(h, b, 1).start()

        def partial(i, target, b):
            seq = bt_ref[target, b]
            slot_lo = jnp.maximum(lo - seq, 0)
            slot_hi = jnp.minimum(lo + 1 + seq, slots - 1)
            scale = SCALE if i == 0 else 1.0
            of_lo = jnp.where(seq <= lo, jnp.float32(scale), jnp.float32(0))
            of_hi = jnp.where(seq <= hi, jnp.float32(scale), jnp.float32(0))
            return (d_slots[i, slot_lo] * of_lo + d_slots[i, slot_hi] * of_hi).T

        for i, left, right in ((1, gg_t, prob), (0, qq_t, dscore)):
            grads = jnp.dot(left[...], right[...], preferred_element_type=jnp.float32)
            for p in range(slots):
                cols = slice(p * BLK, (p + 1) * BLK)
                d_slots[i, p] = pick(p, grads[:HEAD_SIZE, cols], grads[HEAD_SIZE:, cols])
            for b in range(2):
                at = slice(b * BLK, (b + 1) * BLK)
                mate_send[h, i, 0, at] = partial(i, mate, b).astype(jnp.bfloat16)
                mate_send[h, i, 1, at] = partial(i, cross, b).astype(jnp.bfloat16)
            mate_copy(h, i).start()
            for b in range(2):
                at = slice(b * BLK, (b + 1) * BLK)
                y_part[h, i, at] = partial(i, peer, b)
                own_part[h, i, at] = partial(i, me, b)
        second_stage(h, 1)
        return carry

    lax.fori_loop(0, heads, one_head, 0)
    second_stage(heads - 1, 0)

    dkv_copies = []
    for i, dst in ((1, dv_hbm), (0, dk_hbm)):
        for h in range(heads):
            peer_copy(h, i).wait_recv()
            total = (
                own_part[h, i]
                + mate_recv[h, i, 0].astype(jnp.float32)
                + y_recv[h, i].astype(jnp.float32)
            )
            dkv_buf[h, i] = total.astype(jnp.bfloat16)
            copy = pltpu.make_async_copy(
                dkv_buf.at[h, i], dst.at[:, h * HEAD_SIZE : (h + 1) * HEAD_SIZE], dkv_sem.at[h, i]
            )
            copy.start()
            dkv_copies.append(copy)

    for h in range(heads):
        gather_copy(h, me, peer, 0).wait_send()
        gather_copy(h, me, mate, 1).wait_send()
        gather_copy(h, peer, mate, 2).wait_send()
        for i in range(2):
            mate_copy(h, i).wait_send()
            peer_copy(h, i).wait_send()
        for b in range(2):
            out_copy(h, b, 0).wait()
            out_copy(h, b, 1).wait()
    for copy in dkv_copies:
        copy.wait()


def per_device_fused(query_rows, key_rows, stored_value_rows, out_grad, block_table, pattern):
    blocks = pattern.shape[0]
    held, kv_width = key_rows.shape
    heads = kv_width // HEAD_SIZE
    groups = query_rows.shape[1] // kv_width
    width = groups * HEAD_SIZE
    rows = groups * BLK
    slots = blocks + 1
    bf16, f32 = jnp.bfloat16, jnp.float32
    vmem, dma = pltpu.VMEM, pltpu.SemaphoreType.DMA
    ctx = blocks // 2
    pair = 2 * HEAD_SIZE
    scratch = [
        vmem((heads, 2, ctx, held, HEAD_SIZE), bf16),
        vmem((2, blocks, BLK, HEAD_SIZE), bf16),
        vmem((2, BLK, heads * width), bf16),
        vmem((2, BLK, heads * width), bf16),
        vmem((heads, 2, BLK, width), bf16),
        vmem((heads, 2, BLK, width), bf16),
        vmem((rows, pair), bf16),
        vmem((rows, pair), bf16),
        vmem((pair, rows), bf16),
        vmem((pair, rows), bf16),
        vmem((ROWS_CHUNK, pair), bf16),
        vmem((ROWS_CHUNK, pair), bf16),
        vmem((slots * BLK, pair), bf16),
        vmem((slots * BLK, pair), bf16),
        vmem((pair, slots * BLK), bf16),
        vmem((pair, slots * BLK), bf16),
        vmem((2, ROWS_CHUNK, slots * BLK), f32),
        vmem((2, ROWS_CHUNK, slots * BLK), f32),
        vmem((rows, slots * BLK), bf16),
        vmem((rows, slots * BLK), bf16),
        vmem((2, rows, HEAD_SIZE), bf16),
        vmem((2, rows, HEAD_SIZE), bf16),
        vmem((2, slots, HEAD_SIZE, BLK), f32),
        vmem((heads, 2, held, HEAD_SIZE), f32),
        vmem((heads, 2, held, HEAD_SIZE), f32),
        vmem((heads, 2, 2, held, HEAD_SIZE), bf16),
        vmem((heads, 2, 2, held, HEAD_SIZE), bf16),
        vmem((heads, 2, held, HEAD_SIZE), bf16),
        vmem((heads, 2, held, HEAD_SIZE), bf16),
        vmem((heads, 2, held, HEAD_SIZE), bf16),
        dma((2, 2)),
        dma((heads, 2)),
        dma((heads, 2, 2)),
        dma((heads, 2)),
        dma((heads, 3)),
        dma((heads, 3)),
        dma((heads, 2, 2)),
        dma((heads, 2, 2)),
    ]
    smem = pl.BlockSpec(memory_space=pltpu.SMEM)
    hbm = pl.BlockSpec(memory_space=pltpu.HBM)
    return pl.pallas_call(
        functools.partial(fused_kernel, heads, groups, blocks),
        out_shape=(
            jax.ShapeDtypeStruct(query_rows.shape, bf16),
            jax.ShapeDtypeStruct(query_rows.shape, bf16),
            jax.ShapeDtypeStruct(key_rows.shape, bf16),
            jax.ShapeDtypeStruct(key_rows.shape, bf16),
        ),
        in_specs=[smem, smem, hbm, hbm, hbm, hbm],
        out_specs=(hbm, hbm, hbm, hbm),
        scratch_shapes=scratch,
        compiler_params=pltpu.CompilerParams(
            collective_id=0, has_side_effects=True, vmem_limit_bytes=56 * 1024 * 1024
        ),
        cost_estimate=pl.CostEstimate(
            flops=12 * heads * rows * pair * slots * BLK,
            bytes_accessed=8 * query_rows.size + 8 * key_rows.size,
            transcendentals=heads * rows * slots * BLK,
        ),
    )(block_table, pattern, query_rows, key_rows, stored_value_rows, out_grad)


def solution(mesh):
    row_spec = P(("dp", "ctx"), "head")
    in_specs = (row_spec, row_spec, row_spec, row_spec, P("dp", None), P("dp", None))
    out_specs = (row_spec, row_spec, row_spec, row_spec)

    def per_device(query_rows, key_rows, stored_value_rows, out_grad, block_table, pattern):
        fits = mesh.shape["ctx"] == 4 and block_table.shape == (4, 2)
        body = per_device_fused if fits else per_device_wide
        return body(query_rows, key_rows, stored_value_rows, out_grad, block_table, pattern)

    return jax.shard_map(
        per_device, mesh=mesh, in_specs=in_specs, out_specs=out_specs, check_vma=False
    )
```

```python
import functools

import jax
import jax.numpy as jnp
from jax import lax
from jax.experimental import pallas as pl
from jax.experimental.pallas import tpu as pltpu
from jax.sharding import PartitionSpec as P

HEAD_SIZE = 128
BLK = 128
MESH = pl.DeviceIdType.MESH
ROWS_CHUNK = 256
SUB = 32
NEG = -1e30
SCALE = HEAD_SIZE ** (-0.5)
LOG2E = 1.4426950408889634


def slot_layout(block_table, pattern, held_seq):
    blocks = pattern.shape[0]
    slots = pattern.shape[1]
    block_ids = jnp.arange(blocks, dtype=jnp.int32)
    store_seq = block_table.reshape(-1)
    inverse = jnp.sum(
        jnp.where(store_seq[:, None] == block_ids[None, :], block_ids[:, None], 0), axis=0
    )
    onehot = (held_seq[:, None] == block_ids[None, :]).astype(jnp.int32)
    held_pattern = jnp.sum(onehot[:, :, None] * pattern[None, :, :], axis=1)
    key_store = jnp.sum(
        jnp.where(held_pattern[:, :, None] == block_ids[None, None, :], inverse[None, None, :], 0),
        axis=2,
    )
    same = held_pattern[:, :, None] == held_pattern[:, None, :]
    slot_ids = jnp.arange(slots, dtype=jnp.int32)
    before = slot_ids[None, :] < slot_ids[:, None]
    live_slot = jnp.logical_not(jnp.any(same & before[None], axis=2))
    inner = jnp.arange(BLK, dtype=jnp.int32)
    query_pos = held_seq[:, None] * BLK + inner[None, :]
    key_pos = held_pattern[:, :, None] * BLK + inner[None, None, :]
    allowed = live_slot[:, None, :, None] & (key_pos[:, None, :, :] <= query_pos[:, :, None, None])
    return (key_store, allowed)


def attend_tiles(query_held, grad_held, key_tiles, value_tiles, allowed):
    scaling = HEAD_SIZE ** (-0.5)
    scores = (
        jnp.einsum("biagd,bjkad->bagijk", query_held, key_tiles, preferred_element_type=jnp.float32)
        * scaling
    )
    scores = jnp.where(allowed[:, None, None], scores, -jnp.inf)
    row_max = jnp.max(scores, axis=(4, 5), keepdims=True)
    row_sum = jnp.sum(jnp.exp(scores - row_max), axis=(4, 5), keepdims=True)
    log_total = row_max + jnp.log(row_sum)
    prob_full = jnp.exp(scores - log_total)
    prob_low = prob_full.astype(jnp.bfloat16)
    attended_wide = jnp.einsum(
        "bagijk,bjkad->biagd", prob_low, value_tiles, preferred_element_type=jnp.float32
    )
    attended = attended_wide.astype(jnp.bfloat16)
    row_dot = jnp.sum(grad_held.astype(jnp.float32) * attended_wide, axis=-1)
    row_dot = jnp.transpose(row_dot, (0, 2, 3, 1))[..., None, None]
    grad_prob = jnp.einsum(
        "biagd,bjkad->bagijk", grad_held, value_tiles, preferred_element_type=jnp.float32
    )
    grad_score = (prob_full * (grad_prob - row_dot) * scaling).astype(jnp.bfloat16)
    query_grad = jnp.einsum(
        "bagijk,bjkad->biagd", grad_score, key_tiles, preferred_element_type=jnp.float32
    ).astype(jnp.bfloat16)
    key_grads = jnp.einsum(
        "bagijk,biagd->bjkad", grad_score, query_held, preferred_element_type=jnp.float32
    )
    value_grads = jnp.einsum(
        "bagijk,biagd->bjkad", prob_low, grad_held, preferred_element_type=jnp.float32
    )
    return (attended, query_grad, key_grads, value_grads)


def per_device_wide(query_rows, key_rows, stored_value_rows, out_grad, block_table, pattern):
    ctx_index = lax.axis_index("ctx")
    per_dev = block_table.shape[1]
    blocks = pattern.shape[0]
    kv_local = key_rows.shape[1] // HEAD_SIZE
    groups = query_rows.shape[1] // key_rows.shape[1]
    held_rows = per_dev * BLK
    held_seq = lax.dynamic_index_in_dim(block_table, ctx_index, 0, keepdims=False)
    key_store, allowed = slot_layout(block_table, pattern, held_seq)
    key_all, value_all = (
        lax.all_gather(key_rows, "ctx", axis=0, tiled=True),
        lax.all_gather(stored_value_rows, "ctx", axis=0, tiled=True),
    )
    key_blocks = key_all.reshape(blocks, BLK, kv_local, HEAD_SIZE)
    value_blocks = value_all.reshape(blocks, BLK, kv_local, HEAD_SIZE)
    key_tiles = key_blocks[key_store]
    value_tiles = value_blocks[key_store]
    query_held = query_rows.reshape(per_dev, BLK, kv_local, groups, HEAD_SIZE)
    grad_held = out_grad.reshape(per_dev, BLK, kv_local, groups, HEAD_SIZE)
    attended, query_grad, key_grads, value_grads = attend_tiles(
        query_held, grad_held, key_tiles, value_tiles, allowed
    )
    flat_slots = key_store.reshape(-1)

    def scattered(grads):
        partial = (
            jnp.zeros((blocks, BLK, kv_local, HEAD_SIZE), jnp.float32)
            .at[flat_slots]
            .add(grads.reshape(-1, BLK, kv_local, HEAD_SIZE))
        )
        return lax.psum_scatter(
            partial.reshape(blocks * BLK, -1).astype(jnp.bfloat16),
            "ctx",
            scatter_dimension=0,
            tiled=True,
        ).astype(jnp.bfloat16)

    return (
        attended.reshape(held_rows, -1),
        query_grad.reshape(held_rows, -1),
        scattered(key_grads),
        scattered(value_grads),
    )


def fused_kernel(
    heads, groups, blocks,
    bt_ref, pat_ref, q_hbm, k_hbm, v_hbm, g_hbm,
    att_out, dq_out, dk_out, dv_out,
    kv_all, kv_now, q_buf, g_buf,
    qq, gg, qq_t, gg_t, q_scaled, g_scaled, key_slots, value_slots, key_t, value_t, s_buf, d_buf, dv_early, dk_early, prob, dscore, att_now, dq_now,
    d_slots, own_part, y_part, mate_send, mate_recv, y_send, y_recv,
    load_sem, kv_sem, gather_send, gather_recv, red_send, red_recv,
):
    slots = blocks + 1
    half = blocks // 2
    width = groups * HEAD_SIZE
    rows = groups * BLK
    me = lax.axis_index("ctx")
    core, y = me % 2, me // 2
    mate = y * 2 + (1 - core)
    peer = (1 - y) * 2 + core
    cross = (1 - y) * 2 + (1 - core)

    kv_loads = []
    for h in range(heads):
        for i, ref in enumerate((k_hbm, v_hbm)):
            copy = pltpu.make_async_copy(
                ref.at[:, h * HEAD_SIZE : (h + 1) * HEAD_SIZE], kv_all.at[h, i, me], kv_sem.at[h, i]
            )
            copy.start()
            kv_loads.append(copy)
    loads = []
    for i, (src, dst) in enumerate(((q_hbm, q_buf), (g_hbm, g_buf))):
        for b in range(2):
            copy = pltpu.make_async_copy(
                src.at[b * BLK : (b + 1) * BLK], dst.at[b], load_sem.at[i, b]
            )
            copy.start()
            loads.append(copy)

    barrier = pltpu.get_barrier_semaphore()
    for other in (mate, peer):
        pl.semaphore_signal(barrier, inc=1, device_id={"ctx": other}, device_id_type=MESH)
    pl.semaphore_wait(barrier, 2)

    def gather_copy(h, i, source, target, kind):
        return pltpu.make_async_remote_copy(
            src_ref=kv_all.at[h, i, source],
            dst_ref=kv_all.at[h, i, source],
            send_sem=gather_send.at[h, i, kind],
            recv_sem=gather_recv.at[h, i, kind],
            device_id={"ctx": target},
            device_id_type=MESH,
        )

    def gather_arrival(h, i, source, kind):
        return gather_copy(h, i, source, mate, kind)

    def mate_copy(h, i):
        return pltpu.make_async_remote_copy(
            src_ref=mate_send.at[h, i],
            dst_ref=mate_recv.at[h, i],
            send_sem=red_send.at[h, 0, i],
            recv_sem=red_recv.at[h, 0, i],
            device_id={"ctx": mate},
            device_id_type=MESH,
        )

    def peer_copy(h, i):
        return pltpu.make_async_remote_copy(
            src_ref=y_send.at[h, i],
            dst_ref=y_recv.at[h, i],
            send_sem=red_send.at[h, 1, i],
            recv_sem=red_recv.at[h, 1, i],
            device_id={"ctx": peer},
            device_id_type=MESH,
        )

    for h in range(heads):
        for i in range(2):
            kv_loads[2 * h + i].wait()
            gather_copy(h, i, me, peer, 0).start()
            gather_copy(h, i, me, mate, 1).start()

    seq0, seq1 = bt_ref[0, me], bt_ref[1, me]
    lo, hi = jnp.minimum(seq0, seq1), jnp.maximum(seq0, seq1)
    at_lo = jnp.where(seq0 > seq1, 1, 0)
    at_hi = 1 - at_lo
    table = [bt_ref[g % 2, g // 2] for g in range(blocks)]
    homes, biases, is_lo = [], [], []
    for p in range(slots):
        if p == 0:
            mine, key_seq, query_seq = None, lo, lo
        elif p >= half:
            mine, key_seq, query_seq = None, p - lo - 1, hi
        else:
            mine = p <= lo
            key_seq = jnp.where(mine, lo - p, p - lo - 1)
            query_seq = jnp.where(mine, lo, hi)
        home = jnp.int32(0)
        for g in range(blocks):
            home = jnp.where(table[g] == key_seq, g, home)
        homes.append(home)
        is_lo.append(mine)
        if p in (0, slots - 1):
            biases.append(None)
        else:
            hits = jnp.int32(0)
            for j in range(pat_ref.shape[1]):
                hits = hits + jnp.where(pat_ref[query_seq, j] == key_seq, 1, 0)
            biases.append(jnp.where(hits > 0, jnp.float32(0), jnp.float32(NEG)))
    bias_lo = [None if m is None else jnp.where(m, x, NEG) for m, x in zip(is_lo, biases)]
    bias_hi = [None if m is None else jnp.where(m, NEG, x) for m, x in zip(is_lo, biases)]
    in_lo = [None if m is None else jnp.where(m, jnp.float32(1), jnp.float32(0)) for m in is_lo]

    zeros = jnp.zeros((BLK, HEAD_SIZE), jnp.bfloat16)
    for ref, ref_t in ((key_slots, key_t), (value_slots, value_t)):
        for p in range(slots):
            at = slice(p * BLK, (p + 1) * BLK)
            if p == 0:
                ref[at, HEAD_SIZE:] = zeros
                ref_t[HEAD_SIZE:, at] = zeros
            elif p >= half:
                ref[at, :HEAD_SIZE] = zeros
                ref_t[:HEAD_SIZE, at] = zeros

    for copy in loads:
        copy.wait()

    def forward(h, i):
        gather_arrival(h, i, peer, 0).wait_recv()
        gather_copy(h, i, peer, mate, 2).start()

    def second_stage(h, i):
        mate_copy(h, i).wait_recv()
        y_send[h, i] = (y_part[h, i] + mate_recv[h, i, 1].astype(jnp.float32)).astype(jnp.bfloat16)
        peer_copy(h, i).start()

    forward(0, 0)
    forward(0, 1)

    def one_head(h, carry):
        first = pl.multiple_of(h * width, width)
        for src, dst in ((q_buf, qq), (g_buf, gg)):
            for g in range(groups):
                cols = pl.ds(pl.multiple_of(first + g * HEAD_SIZE, HEAD_SIZE), HEAD_SIZE)
                for part, at in ((0, at_lo), (1, at_hi)):
                    tile = src[at, :, cols]
                    dst[g * BLK : (g + 1) * BLK, part * HEAD_SIZE : (part + 1) * HEAD_SIZE] = tile

        for i in range(2):
            gather_arrival(h, i, mate, 1).wait_recv()
            gather_arrival(h, i, cross, 2).wait_recv()
        for i in range(2):
            for c in range(blocks // 2):
                for b in range(2):
                    kv_now[i, c * 2 + b] = kv_all[h, i, c, b * BLK : (b + 1) * BLK]
        for i, (ref, ref_t) in enumerate(((key_slots, key_t), (value_slots, value_t))):
            for p in range(slots):
                tile = kv_now[i, homes[p]]
                tile_t = tile.T
                at = slice(p * BLK, (p + 1) * BLK)
                if p == 0:
                    ref[at, :HEAD_SIZE] = tile
                    ref_t[:HEAD_SIZE, at] = tile_t
                elif p >= half:
                    ref[at, HEAD_SIZE:] = tile
                    ref_t[HEAD_SIZE:, at] = tile_t
                else:
                    for target, index, value in (
                        (ref, (at, slice(0, HEAD_SIZE)), tile),
                        (ref_t, (slice(0, HEAD_SIZE), at), tile_t),
                    ):
                        wide = value.astype(jnp.float32)
                        target[index] = (wide * in_lo[p]).astype(jnp.bfloat16)
                    for target, index, value in (
                        (ref, (at, slice(HEAD_SIZE, None)), tile),
                        (ref_t, (slice(HEAD_SIZE, None), at), tile_t),
                    ):
                        wide = value.astype(jnp.float32)
                        target[index] = (wide * (1.0 - in_lo[p])).astype(jnp.bfloat16)

        def matmuls(c):
            at = slice(c * ROWS_CHUNK, (c + 1) * ROWS_CHUNK)
            s_buf[c % 2] = jnp.dot(qq[at, :], key_t[...], preferred_element_type=jnp.float32)
            d_buf[c % 2] = jnp.dot(gg[at, :], value_t[...], preferred_element_type=jnp.float32)

        def pick(p, of_lo, of_hi):
            if p == 0:
                return of_lo
            if p >= half:
                return of_hi
            return jnp.where(is_lo[p], of_lo, of_hi)

        def softmax(c, r):
            rows_at = slice(c * ROWS_CHUNK + r, c * ROWS_CHUNK + r + SUB)
            inner = slice(r, r + SUB)
            row = lax.broadcasted_iota(jnp.int32, (SUB, BLK), 0) + (c * ROWS_CHUNK + r) % BLK
            col = lax.broadcasted_iota(jnp.int32, (SUB, BLK), 1)
            tiles = [s_buf[c % 2, inner, p * BLK : (p + 1) * BLK] for p in range(slots)]
            for p in (0, slots - 1):
                tiles[p] = jnp.where(col <= row, tiles[p], NEG)
            max_lo, max_hi = tiles[0], tiles[slots - 1]
            for p in range(1, slots - 1):
                if p < half:
                    max_lo = jnp.maximum(max_lo, tiles[p] + bias_lo[p])
                    max_hi = jnp.maximum(max_hi, tiles[p] + bias_hi[p])
                else:
                    max_hi = jnp.maximum(max_hi, tiles[p] + biases[p])
            max_lo = jnp.max(max_lo, axis=1, keepdims=True)
            max_hi = jnp.max(max_hi, axis=1, keepdims=True)
            sum_lo = sum_hi = None
            for p in range(slots):
                top = pick(p, max_lo, max_hi)
                if biases[p] is not None:
                    top = top - biases[p]
                tile = jnp.exp2((tiles[p] - top) * (SCALE * LOG2E))
                s_buf[c % 2, inner, p * BLK : (p + 1) * BLK] = tile
                prob[rows_at, p * BLK : (p + 1) * BLK] = tile.astype(jnp.bfloat16)
                if p == 0:
                    sum_lo = tile
                elif p < half:
                    sum_lo = sum_lo + jnp.where(is_lo[p], tile, 0.0)
                    part = jnp.where(is_lo[p], 0.0, tile)
                    sum_hi = part if sum_hi is None else sum_hi + part
                else:
                    sum_hi = tile if sum_hi is None else sum_hi + tile
            inv_lo = 1.0 / jnp.sum(sum_lo, axis=1, keepdims=True)
            inv_hi = 1.0 / jnp.sum(sum_hi, axis=1, keepdims=True)
            for src, dst in ((qq, q_scaled), (gg, g_scaled)):
                for cols, inv in ((slice(0, HEAD_SIZE), inv_lo), (slice(HEAD_SIZE, None), inv_hi)):
                    dst[inner, cols] = (src[rows_at, cols].astype(jnp.float32) * inv).astype(
                        jnp.bfloat16
                    )
            return inv_lo, inv_hi

        def finish(c):
            at = slice(c * ROWS_CHUNK, (c + 1) * ROWS_CHUNK)
            inverses = [softmax(c, r) for r in range(0, ROWS_CHUNK, SUB)]
            wide = jnp.dot(prob[at, :], value_slots[...], preferred_element_type=jnp.float32)
            for src, dst in ((q_scaled, qq_t), (g_scaled, gg_t)):
                dst[:, at] = src[...].T
            for n, (inv_lo, inv_hi) in enumerate(inverses):
                inner = slice(n * SUB, (n + 1) * SUB)
                rows_at = slice(c * ROWS_CHUNK + n * SUB, c * ROWS_CHUNK + (n + 1) * SUB)
                of_lo = wide[inner, :HEAD_SIZE] * inv_lo
                of_hi = wide[inner, HEAD_SIZE:] * inv_hi
                att_now[0, rows_at, :] = of_lo.astype(jnp.bfloat16)
                att_now[1, rows_at, :] = of_hi.astype(jnp.bfloat16)
                grad = gg[rows_at, :].astype(jnp.float32)
                dot_lo = jnp.sum(of_lo * grad[:, :HEAD_SIZE], axis=1, keepdims=True)
                dot_hi = jnp.sum(of_hi * grad[:, HEAD_SIZE:], axis=1, keepdims=True)
                for p in range(slots):
                    cols = slice(p * BLK, (p + 1) * BLK)
                    dscore[rows_at, cols] = (
                        s_buf[c % 2, inner, cols]
                        * (d_buf[c % 2, inner, cols] - pick(p, dot_lo, dot_hi))
                    ).astype(jnp.bfloat16)
            dq = jnp.dot(dscore[at, :], key_slots[...], preferred_element_type=jnp.float32)
            for n, (inv_lo, inv_hi) in enumerate(inverses):
                inner = slice(n * SUB, (n + 1) * SUB)
                rows_at = slice(c * ROWS_CHUNK + n * SUB, c * ROWS_CHUNK + (n + 1) * SUB)
                dq_now[0, rows_at, :] = (dq[inner, :HEAD_SIZE] * (inv_lo * SCALE)).astype(
                    jnp.bfloat16
                )
                dq_now[1, rows_at, :] = (dq[inner, HEAD_SIZE:] * (inv_hi * SCALE)).astype(
                    jnp.bfloat16
                )

        chunks = rows // ROWS_CHUNK
        early = slice(0, rows // 2)
        matmuls(0)
        for c in range(chunks):
            if c + 1 < chunks:
                matmuls(c + 1)
            if c == chunks // 2:
                dv_early[...] = jnp.dot(
                    gg_t[:, early], prob[early, :], preferred_element_type=jnp.float32
                )
            if c == chunks - 1:
                dk_early[...] = jnp.dot(
                    qq_t[:, early], dscore[early, :], preferred_element_type=jnp.float32
                )
            finish(c)

        @pl.when(h < heads - 1)
        def _():
            forward(h + 1, 0)
            forward(h + 1, 1)

        @pl.when(h > 0)
        def _():
            second_stage(h - 1, 0)

        for b in range(2):
            from_now = jnp.where(at_lo == b, 0, 1)
            at = slice(b * BLK, (b + 1) * BLK)
            for g in range(groups):
                cols = pl.ds(pl.multiple_of(first + g * HEAD_SIZE, HEAD_SIZE), HEAD_SIZE)
                att_out[at, cols] = att_now[from_now, g * BLK : (g + 1) * BLK, :]
                dq_out[at, cols] = dq_now[from_now, g * BLK : (g + 1) * BLK, :]

        def partial(i, target, b):
            seq = bt_ref[b, target]
            slot_lo = jnp.maximum(lo - seq, 0)
            slot_hi = jnp.minimum(lo + 1 + seq, slots - 1)
            scale = SCALE if i == 0 else 1.0
            of_lo = jnp.where(seq <= lo, jnp.float32(scale), jnp.float32(0))
            of_hi = jnp.where(seq <= hi, jnp.float32(scale), jnp.float32(0))
            return (d_slots[i, slot_lo] * of_lo + d_slots[i, slot_hi] * of_hi).T

        late = slice(rows // 2, rows)
        for i, left, right, first_half in (
            (1, gg_t, prob, dv_early),
            (0, qq_t, dscore, dk_early),
        ):
            grads = first_half[...] + jnp.dot(
                left[:, late], right[late, :], preferred_element_type=jnp.float32
            )
            for p in range(slots):
                cols = slice(p * BLK, (p + 1) * BLK)
                d_slots[i, p] = pick(p, grads[:HEAD_SIZE, cols], grads[HEAD_SIZE:, cols])
            for b in range(2):
                at = slice(b * BLK, (b + 1) * BLK)
                mate_send[h, i, 0, at] = partial(i, mate, b).astype(jnp.bfloat16)
                mate_send[h, i, 1, at] = partial(i, cross, b).astype(jnp.bfloat16)
            mate_copy(h, i).start()
            for b in range(2):
                at = slice(b * BLK, (b + 1) * BLK)
                y_part[h, i, at] = partial(i, peer, b)
                own_part[h, i, at] = partial(i, me, b)
        second_stage(h, 1)
        return carry

    lax.fori_loop(0, heads, one_head, 0)
    second_stage(heads - 1, 0)

    for i, dst in ((1, dv_out), (0, dk_out)):
        for h in range(heads):
            peer_copy(h, i).wait_recv()
            total = (
                own_part[h, i]
                + mate_recv[h, i, 0].astype(jnp.float32)
                + y_recv[h, i].astype(jnp.float32)
            )
            dst[:, h * HEAD_SIZE : (h + 1) * HEAD_SIZE] = total.astype(jnp.bfloat16)

    for h in range(heads):
        for i in range(2):
            gather_copy(h, i, me, peer, 0).wait_send()
            gather_copy(h, i, me, mate, 1).wait_send()
            gather_copy(h, i, peer, mate, 2).wait_send()
            mate_copy(h, i).wait_send()
            peer_copy(h, i).wait_send()


def write_kernel(*refs):
    copies = [
        pltpu.make_async_copy(refs[i], refs[4 + i], refs[8].at[i]) for i in range(4)
    ]
    for copy in copies:
        copy.start()
    for copy in copies:
        copy.wait()


def per_device_fused(query_rows, key_rows, stored_value_rows, out_grad, block_table, pattern):
    blocks = pattern.shape[0]
    held, kv_width = key_rows.shape
    heads = kv_width // HEAD_SIZE
    groups = query_rows.shape[1] // kv_width
    width = groups * HEAD_SIZE
    rows = groups * BLK
    slots = blocks + 1
    bf16, f32 = jnp.bfloat16, jnp.float32
    vmem, dma = pltpu.VMEM, pltpu.SemaphoreType.DMA
    ctx = blocks // 2
    pair = 2 * HEAD_SIZE
    scratch = [
        vmem((heads, 2, ctx, held, HEAD_SIZE), bf16),
        vmem((2, blocks, BLK, HEAD_SIZE), bf16),
        vmem((2, BLK, heads * width), bf16),
        vmem((2, BLK, heads * width), bf16),
        vmem((rows, pair), bf16),
        vmem((rows, pair), bf16),
        vmem((pair, rows), bf16),
        vmem((pair, rows), bf16),
        vmem((ROWS_CHUNK, pair), bf16),
        vmem((ROWS_CHUNK, pair), bf16),
        vmem((slots * BLK, pair), bf16),
        vmem((slots * BLK, pair), bf16),
        vmem((pair, slots * BLK), bf16),
        vmem((pair, slots * BLK), bf16),
        vmem((2, ROWS_CHUNK, slots * BLK), f32),
        vmem((2, ROWS_CHUNK, slots * BLK), f32),
        vmem((pair, slots * BLK), f32),
        vmem((pair, slots * BLK), f32),
        vmem((rows, slots * BLK), bf16),
        vmem((rows, slots * BLK), bf16),
        vmem((2, rows, HEAD_SIZE), bf16),
        vmem((2, rows, HEAD_SIZE), bf16),
        vmem((2, slots, HEAD_SIZE, BLK), f32),
        vmem((heads, 2, held, HEAD_SIZE), f32),
        vmem((heads, 2, held, HEAD_SIZE), f32),
        vmem((heads, 2, 2, held, HEAD_SIZE), bf16),
        vmem((heads, 2, 2, held, HEAD_SIZE), bf16),
        vmem((heads, 2, held, HEAD_SIZE), bf16),
        vmem((heads, 2, held, HEAD_SIZE), bf16),
        dma((2, 2)),
        dma((heads, 2)),
        dma((heads, 2, 3)),
        dma((heads, 2, 3)),
        dma((heads, 2, 2)),
        dma((heads, 2, 2)),
    ]
    smem = pl.BlockSpec(memory_space=pltpu.SMEM)
    hbm = pl.BlockSpec(memory_space=pltpu.HBM)
    on_chip = pl.BlockSpec(memory_space=pltpu.VMEM)
    out_shapes = (query_rows.shape, query_rows.shape, key_rows.shape, key_rows.shape)
    results = pl.pallas_call(
        functools.partial(fused_kernel, heads, groups, blocks),
        out_shape=tuple(vmem(shape, bf16) for shape in out_shapes),
        in_specs=[smem, smem, hbm, hbm, hbm, hbm],
        out_specs=(on_chip,) * 4,
        scratch_shapes=scratch,
        compiler_params=pltpu.CompilerParams(
            collective_id=0, has_side_effects=True, vmem_limit_bytes=48 * 1024 * 1024
        ),
        cost_estimate=pl.CostEstimate(
            flops=12 * heads * rows * pair * slots * BLK,
            bytes_accessed=8 * query_rows.size + 8 * key_rows.size,
            transcendentals=heads * rows * slots * BLK,
        ),
    )(block_table.T, pattern, query_rows, key_rows, stored_value_rows, out_grad)
    return pl.pallas_call(
        write_kernel,
        out_shape=tuple(jax.ShapeDtypeStruct(shape, bf16) for shape in out_shapes),
        in_specs=[on_chip] * 4,
        out_specs=(hbm,) * 4,
        scratch_shapes=[dma((4,))],
    )(*results)


def solution(mesh):
    row_spec = P(("dp", "ctx"), "head")
    in_specs = (row_spec, row_spec, row_spec, row_spec, P("dp", None), P("dp", None))
    out_specs = (row_spec, row_spec, row_spec, row_spec)

    def per_device(query_rows, key_rows, stored_value_rows, out_grad, block_table, pattern):
        fits = mesh.shape["ctx"] == 4 and block_table.shape == (4, 2)
        body = per_device_fused if fits else per_device_wide
        return body(query_rows, key_rows, stored_value_rows, out_grad, block_table, pattern)

    return jax.shard_map(
        per_device, mesh=mesh, in_specs=in_specs, out_specs=out_specs, check_vma=False
    )
```

```python
import functools

import jax
import jax.numpy as jnp
from jax import lax
from jax.experimental import pallas as pl
from jax.experimental.pallas import tpu as pltpu
from jax.sharding import PartitionSpec as P

HEAD_SIZE = 128
BLK = 128
MESH = pl.DeviceIdType.MESH
ROWS_CHUNK = 512
SUB = 32
NEG = -1e30
SCALE = HEAD_SIZE ** (-0.5)
LOG2E = 1.4426950408889634


def slot_layout(block_table, pattern, held_seq):
    blocks = pattern.shape[0]
    slots = pattern.shape[1]
    block_ids = jnp.arange(blocks, dtype=jnp.int32)
    store_seq = block_table.reshape(-1)
    inverse = jnp.sum(
        jnp.where(store_seq[:, None] == block_ids[None, :], block_ids[:, None], 0), axis=0
    )
    onehot = (held_seq[:, None] == block_ids[None, :]).astype(jnp.int32)
    held_pattern = jnp.sum(onehot[:, :, None] * pattern[None, :, :], axis=1)
    key_store = jnp.sum(
        jnp.where(held_pattern[:, :, None] == block_ids[None, None, :], inverse[None, None, :], 0),
        axis=2,
    )
    same = held_pattern[:, :, None] == held_pattern[:, None, :]
    slot_ids = jnp.arange(slots, dtype=jnp.int32)
    before = slot_ids[None, :] < slot_ids[:, None]
    live_slot = jnp.logical_not(jnp.any(same & before[None], axis=2))
    inner = jnp.arange(BLK, dtype=jnp.int32)
    query_pos = held_seq[:, None] * BLK + inner[None, :]
    key_pos = held_pattern[:, :, None] * BLK + inner[None, None, :]
    allowed = live_slot[:, None, :, None] & (key_pos[:, None, :, :] <= query_pos[:, :, None, None])
    return (key_store, allowed)


def attend_tiles(query_held, grad_held, key_tiles, value_tiles, allowed):
    scaling = HEAD_SIZE ** (-0.5)
    scores = (
        jnp.einsum("biagd,bjkad->bagijk", query_held, key_tiles, preferred_element_type=jnp.float32)
        * scaling
    )
    scores = jnp.where(allowed[:, None, None], scores, -jnp.inf)
    row_max = jnp.max(scores, axis=(4, 5), keepdims=True)
    row_sum = jnp.sum(jnp.exp(scores - row_max), axis=(4, 5), keepdims=True)
    log_total = row_max + jnp.log(row_sum)
    prob_full = jnp.exp(scores - log_total)
    prob_low = prob_full.astype(jnp.bfloat16)
    attended_wide = jnp.einsum(
        "bagijk,bjkad->biagd", prob_low, value_tiles, preferred_element_type=jnp.float32
    )
    attended = attended_wide.astype(jnp.bfloat16)
    row_dot = jnp.sum(grad_held.astype(jnp.float32) * attended_wide, axis=-1)
    row_dot = jnp.transpose(row_dot, (0, 2, 3, 1))[..., None, None]
    grad_prob = jnp.einsum(
        "biagd,bjkad->bagijk", grad_held, value_tiles, preferred_element_type=jnp.float32
    )
    grad_score = (prob_full * (grad_prob - row_dot) * scaling).astype(jnp.bfloat16)
    query_grad = jnp.einsum(
        "bagijk,bjkad->biagd", grad_score, key_tiles, preferred_element_type=jnp.float32
    ).astype(jnp.bfloat16)
    key_grads = jnp.einsum(
        "bagijk,biagd->bjkad", grad_score, query_held, preferred_element_type=jnp.float32
    )
    value_grads = jnp.einsum(
        "bagijk,biagd->bjkad", prob_low, grad_held, preferred_element_type=jnp.float32
    )
    return (attended, query_grad, key_grads, value_grads)


def per_device_wide(query_rows, key_rows, stored_value_rows, out_grad, block_table, pattern):
    ctx_index = lax.axis_index("ctx")
    per_dev = block_table.shape[1]
    blocks = pattern.shape[0]
    kv_local = key_rows.shape[1] // HEAD_SIZE
    groups = query_rows.shape[1] // key_rows.shape[1]
    held_rows = per_dev * BLK
    held_seq = lax.dynamic_index_in_dim(block_table, ctx_index, 0, keepdims=False)
    key_store, allowed = slot_layout(block_table, pattern, held_seq)
    key_all, value_all = (
        lax.all_gather(key_rows, "ctx", axis=0, tiled=True),
        lax.all_gather(stored_value_rows, "ctx", axis=0, tiled=True),
    )
    key_blocks = key_all.reshape(blocks, BLK, kv_local, HEAD_SIZE)
    value_blocks = value_all.reshape(blocks, BLK, kv_local, HEAD_SIZE)
    key_tiles = key_blocks[key_store]
    value_tiles = value_blocks[key_store]
    query_held = query_rows.reshape(per_dev, BLK, kv_local, groups, HEAD_SIZE)
    grad_held = out_grad.reshape(per_dev, BLK, kv_local, groups, HEAD_SIZE)
    attended, query_grad, key_grads, value_grads = attend_tiles(
        query_held, grad_held, key_tiles, value_tiles, allowed
    )
    flat_slots = key_store.reshape(-1)

    def scattered(grads):
        partial = (
            jnp.zeros((blocks, BLK, kv_local, HEAD_SIZE), jnp.float32)
            .at[flat_slots]
            .add(grads.reshape(-1, BLK, kv_local, HEAD_SIZE))
        )
        return lax.psum_scatter(
            partial.reshape(blocks * BLK, -1).astype(jnp.bfloat16),
            "ctx",
            scatter_dimension=0,
            tiled=True,
        ).astype(jnp.bfloat16)

    return (
        attended.reshape(held_rows, -1),
        query_grad.reshape(held_rows, -1),
        scattered(key_grads),
        scattered(value_grads),
    )


def fused_kernel(
    heads, groups, blocks,
    bt_ref, pat_ref, q_hbm, k_hbm, v_hbm, g_hbm,
    att_hbm, dq_hbm, dk_hbm, dv_hbm,
    kv_all, kv_now, q_buf, g_buf, att_buf, dq_buf,
    qq, gg, qq_t, gg_t, q_scaled, g_scaled, key_slots, value_slots, key_t, value_t, s_buf, d_buf, dv_early, dk_early, prob, dscore, att_now, dq_now,
    d_slots, own_part, y_part, mate_send, mate_recv, y_send, y_recv, dkv_buf,
    load_sem, kv_sem, out_sem, dkv_sem, gather_send, gather_recv, red_send, red_recv,
):
    slots = blocks + 1
    half = blocks // 2
    width = groups * HEAD_SIZE
    rows = groups * BLK
    me = lax.axis_index("ctx")
    core, y = me % 2, me // 2
    mate = y * 2 + (1 - core)
    peer = (1 - y) * 2 + core
    cross = (1 - y) * 2 + (1 - core)

    kv_loads = []
    for h in range(heads):
        for i, ref in enumerate((k_hbm, v_hbm)):
            copy = pltpu.make_async_copy(
                ref.at[:, h * HEAD_SIZE : (h + 1) * HEAD_SIZE], kv_all.at[h, i, me], kv_sem.at[h, i]
            )
            copy.start()
            kv_loads.append(copy)
    loads = []
    for i, (src, dst) in enumerate(((q_hbm, q_buf), (g_hbm, g_buf))):
        for b in range(2):
            copy = pltpu.make_async_copy(
                src.at[b * BLK : (b + 1) * BLK], dst.at[b], load_sem.at[i, b]
            )
            copy.start()
            loads.append(copy)

    barrier = pltpu.get_barrier_semaphore()
    for other in (mate, peer):
        pl.semaphore_signal(barrier, inc=1, device_id={"ctx": other}, device_id_type=MESH)
    pl.semaphore_wait(barrier, 2)

    def gather_copy(h, i, source, target, kind):
        return pltpu.make_async_remote_copy(
            src_ref=kv_all.at[h, i, source],
            dst_ref=kv_all.at[h, i, source],
            send_sem=gather_send.at[h, i, kind],
            recv_sem=gather_recv.at[h, i, kind],
            device_id={"ctx": target},
            device_id_type=MESH,
        )

    def gather_arrival(h, i, source, kind):
        return gather_copy(h, i, source, mate, kind)

    def mate_copy(h, i):
        return pltpu.make_async_remote_copy(
            src_ref=mate_send.at[h, i],
            dst_ref=mate_recv.at[h, i],
            send_sem=red_send.at[h, 0, i],
            recv_sem=red_recv.at[h, 0, i],
            device_id={"ctx": mate},
            device_id_type=MESH,
        )

    def peer_copy(h, i):
        return pltpu.make_async_remote_copy(
            src_ref=y_send.at[h, i],
            dst_ref=y_recv.at[h, i],
            send_sem=red_send.at[h, 1, i],
            recv_sem=red_recv.at[h, 1, i],
            device_id={"ctx": peer},
            device_id_type=MESH,
        )

    def out_copy(h, b, i):
        buf, dst = ((att_buf, att_hbm), (dq_buf, dq_hbm))[i]
        return pltpu.make_async_copy(
            buf.at[h, b],
            dst.at[b * BLK : (b + 1) * BLK, pl.ds(pl.multiple_of(h * width, width), width)],
            out_sem.at[h, b, i],
        )

    for h in range(heads):
        for i in range(2):
            kv_loads[2 * h + i].wait()
            gather_copy(h, i, me, peer, 0).start()
            gather_copy(h, i, me, mate, 1).start()

    seq0, seq1 = bt_ref[0, me], bt_ref[1, me]
    lo, hi = jnp.minimum(seq0, seq1), jnp.maximum(seq0, seq1)
    at_lo = jnp.where(seq0 > seq1, 1, 0)
    at_hi = 1 - at_lo
    table = [bt_ref[g % 2, g // 2] for g in range(blocks)]
    homes, biases, is_lo = [], [], []
    for p in range(slots):
        if p == 0:
            mine, key_seq, query_seq = None, lo, lo
        elif p >= half:
            mine, key_seq, query_seq = None, p - lo - 1, hi
        else:
            mine = p <= lo
            key_seq = jnp.where(mine, lo - p, p - lo - 1)
            query_seq = jnp.where(mine, lo, hi)
        home = jnp.int32(0)
        for g in range(blocks):
            home = jnp.where(table[g] == key_seq, g, home)
        homes.append(home)
        is_lo.append(mine)
        if p in (0, slots - 1):
            biases.append(None)
        else:
            hits = jnp.int32(0)
            for j in range(pat_ref.shape[1]):
                hits = hits + jnp.where(pat_ref[query_seq, j] == key_seq, 1, 0)
            biases.append(jnp.where(hits > 0, jnp.float32(0), jnp.float32(NEG)))
    bias_lo = [None if m is None else jnp.where(m, x, NEG) for m, x in zip(is_lo, biases)]
    bias_hi = [None if m is None else jnp.where(m, NEG, x) for m, x in zip(is_lo, biases)]
    in_lo = [None if m is None else jnp.where(m, jnp.float32(1), jnp.float32(0)) for m in is_lo]

    zeros = jnp.zeros((BLK, HEAD_SIZE), jnp.bfloat16)
    for ref, ref_t in ((key_slots, key_t), (value_slots, value_t)):
        for p in range(slots):
            at = slice(p * BLK, (p + 1) * BLK)
            if p == 0:
                ref[at, HEAD_SIZE:] = zeros
                ref_t[HEAD_SIZE:, at] = zeros
            elif p >= half:
                ref[at, :HEAD_SIZE] = zeros
                ref_t[:HEAD_SIZE, at] = zeros

    for copy in loads:
        copy.wait()

    def forward(h, i):
        gather_arrival(h, i, peer, 0).wait_recv()
        gather_copy(h, i, peer, mate, 2).start()

    def second_stage(h, i):
        mate_copy(h, i).wait_recv()
        y_send[h, i] = (y_part[h, i] + mate_recv[h, i, 1].astype(jnp.float32)).astype(jnp.bfloat16)
        peer_copy(h, i).start()

    forward(0, 0)
    forward(0, 1)

    def one_head(h, carry):
        first = pl.multiple_of(h * width, width)
        for src, dst in ((q_buf, qq), (g_buf, gg)):
            for g in range(groups):
                cols = pl.ds(pl.multiple_of(first + g * HEAD_SIZE, HEAD_SIZE), HEAD_SIZE)
                for part, at in ((0, at_lo), (1, at_hi)):
                    tile = src[at, :, cols]
                    dst[g * BLK : (g + 1) * BLK, part * HEAD_SIZE : (part + 1) * HEAD_SIZE] = tile

        for i in range(2):
            gather_arrival(h, i, mate, 1).wait_recv()
            gather_arrival(h, i, cross, 2).wait_recv()
        for i in range(2):
            for c in range(blocks // 2):
                for b in range(2):
                    kv_now[i, c * 2 + b] = kv_all[h, i, c, b * BLK : (b + 1) * BLK]
        for i, (ref, ref_t) in enumerate(((key_slots, key_t), (value_slots, value_t))):
            for p in range(slots):
                tile = kv_now[i, homes[p]]
                tile_t = tile.T
                at = slice(p * BLK, (p + 1) * BLK)
                if p == 0:
                    ref[at, :HEAD_SIZE] = tile
                    ref_t[:HEAD_SIZE, at] = tile_t
                elif p >= half:
                    ref[at, HEAD_SIZE:] = tile
                    ref_t[HEAD_SIZE:, at] = tile_t
                else:
                    for target, index, value in (
                        (ref, (at, slice(0, HEAD_SIZE)), tile),
                        (ref_t, (slice(0, HEAD_SIZE), at), tile_t),
                    ):
                        wide = value.astype(jnp.float32)
                        target[index] = (wide * in_lo[p]).astype(jnp.bfloat16)
                    for target, index, value in (
                        (ref, (at, slice(HEAD_SIZE, None)), tile),
                        (ref_t, (slice(HEAD_SIZE, None), at), tile_t),
                    ):
                        wide = value.astype(jnp.float32)
                        target[index] = (wide * (1.0 - in_lo[p])).astype(jnp.bfloat16)

        def matmuls(c):
            at = slice(c * ROWS_CHUNK, (c + 1) * ROWS_CHUNK)
            s_buf[c % 2] = jnp.dot(qq[at, :], key_t[...], preferred_element_type=jnp.float32)
            d_buf[c % 2] = jnp.dot(gg[at, :], value_t[...], preferred_element_type=jnp.float32)

        def pick(p, of_lo, of_hi):
            if p == 0:
                return of_lo
            if p >= half:
                return of_hi
            return jnp.where(is_lo[p], of_lo, of_hi)

        def softmax(c, r):
            rows_at = slice(c * ROWS_CHUNK + r, c * ROWS_CHUNK + r + SUB)
            inner = slice(r, r + SUB)
            row = lax.broadcasted_iota(jnp.int32, (SUB, BLK), 0) + (c * ROWS_CHUNK + r) % BLK
            col = lax.broadcasted_iota(jnp.int32, (SUB, BLK), 1)
            tiles = [s_buf[c % 2, inner, p * BLK : (p + 1) * BLK] for p in range(slots)]
            for p in (0, slots - 1):
                tiles[p] = jnp.where(col <= row, tiles[p], NEG)
            max_lo, max_hi = tiles[0], tiles[slots - 1]
            for p in range(1, slots - 1):
                if p < half:
                    max_lo = jnp.maximum(max_lo, tiles[p] + bias_lo[p])
                    max_hi = jnp.maximum(max_hi, tiles[p] + bias_hi[p])
                else:
                    max_hi = jnp.maximum(max_hi, tiles[p] + biases[p])
            max_lo = jnp.max(max_lo, axis=1, keepdims=True)
            max_hi = jnp.max(max_hi, axis=1, keepdims=True)
            sum_lo = sum_hi = None
            for p in range(slots):
                top = pick(p, max_lo, max_hi)
                if biases[p] is not None:
                    top = top - biases[p]
                tile = jnp.exp2((tiles[p] - top) * (SCALE * LOG2E))
                s_buf[c % 2, inner, p * BLK : (p + 1) * BLK] = tile
                prob[rows_at, p * BLK : (p + 1) * BLK] = tile.astype(jnp.bfloat16)
                if p == 0:
                    sum_lo = tile
                elif p < half:
                    sum_lo = sum_lo + jnp.where(is_lo[p], tile, 0.0)
                    part = jnp.where(is_lo[p], 0.0, tile)
                    sum_hi = part if sum_hi is None else sum_hi + part
                else:
                    sum_hi = tile if sum_hi is None else sum_hi + tile
            inv_lo = 1.0 / jnp.sum(sum_lo, axis=1, keepdims=True)
            inv_hi = 1.0 / jnp.sum(sum_hi, axis=1, keepdims=True)
            for src, dst in ((qq, q_scaled), (gg, g_scaled)):
                for cols, inv in ((slice(0, HEAD_SIZE), inv_lo), (slice(HEAD_SIZE, None), inv_hi)):
                    dst[inner, cols] = (src[rows_at, cols].astype(jnp.float32) * inv).astype(
                        jnp.bfloat16
                    )
            return inv_lo, inv_hi

        def finish(c):
            at = slice(c * ROWS_CHUNK, (c + 1) * ROWS_CHUNK)
            inverses = [softmax(c, r) for r in range(0, ROWS_CHUNK, SUB)]
            wide = jnp.dot(prob[at, :], value_slots[...], preferred_element_type=jnp.float32)
            for src, dst in ((q_scaled, qq_t), (g_scaled, gg_t)):
                dst[:, at] = src[...].T
            for n, (inv_lo, inv_hi) in enumerate(inverses):
                inner = slice(n * SUB, (n + 1) * SUB)
                rows_at = slice(c * ROWS_CHUNK + n * SUB, c * ROWS_CHUNK + (n + 1) * SUB)
                of_lo = wide[inner, :HEAD_SIZE] * inv_lo
                of_hi = wide[inner, HEAD_SIZE:] * inv_hi
                att_now[0, rows_at, :] = of_lo.astype(jnp.bfloat16)
                att_now[1, rows_at, :] = of_hi.astype(jnp.bfloat16)
                grad = gg[rows_at, :].astype(jnp.float32)
                dot_lo = jnp.sum(of_lo * grad[:, :HEAD_SIZE], axis=1, keepdims=True)
                dot_hi = jnp.sum(of_hi * grad[:, HEAD_SIZE:], axis=1, keepdims=True)
                for p in range(slots):
                    cols = slice(p * BLK, (p + 1) * BLK)
                    dscore[rows_at, cols] = (
                        s_buf[c % 2, inner, cols]
                        * (d_buf[c % 2, inner, cols] - pick(p, dot_lo, dot_hi))
                    ).astype(jnp.bfloat16)
            dq = jnp.dot(dscore[at, :], key_slots[...], preferred_element_type=jnp.float32)
            for n, (inv_lo, inv_hi) in enumerate(inverses):
                inner = slice(n * SUB, (n + 1) * SUB)
                rows_at = slice(c * ROWS_CHUNK + n * SUB, c * ROWS_CHUNK + (n + 1) * SUB)
                dq_now[0, rows_at, :] = (dq[inner, :HEAD_SIZE] * (inv_lo * SCALE)).astype(
                    jnp.bfloat16
                )
                dq_now[1, rows_at, :] = (dq[inner, HEAD_SIZE:] * (inv_hi * SCALE)).astype(
                    jnp.bfloat16
                )

        chunks = rows // ROWS_CHUNK
        early = slice(0, rows // 2)
        matmuls(0)
        for c in range(chunks):
            if c + 1 < chunks:
                matmuls(c + 1)
            if c == chunks // 2:
                dv_early[...] = jnp.dot(
                    gg_t[:, early], prob[early, :], preferred_element_type=jnp.float32
                )
            if c == chunks - 1:
                dk_early[...] = jnp.dot(
                    qq_t[:, early], dscore[early, :], preferred_element_type=jnp.float32
                )
            finish(c)

        @pl.when(h < heads - 1)
        def _():
            forward(h + 1, 0)
            forward(h + 1, 1)

        @pl.when(h > 0)
        def _():
            second_stage(h - 1, 0)

        for b in range(2):
            from_now = jnp.where(at_lo == b, 0, 1)
            for g in range(groups):
                cols = slice(g * HEAD_SIZE, (g + 1) * HEAD_SIZE)
                att_buf[h, b, :, cols] = att_now[from_now, g * BLK : (g + 1) * BLK, :]
                dq_buf[h, b, :, cols] = dq_now[from_now, g * BLK : (g + 1) * BLK, :]
            out_copy(h, b, 0).start()
            out_copy(h, b, 1).start()

        def partial(i, target, b):
            seq = bt_ref[b, target]
            slot_lo = jnp.maximum(lo - seq, 0)
            slot_hi = jnp.minimum(lo + 1 + seq, slots - 1)
            scale = SCALE if i == 0 else 1.0
            of_lo = jnp.where(seq <= lo, jnp.float32(scale), jnp.float32(0))
            of_hi = jnp.where(seq <= hi, jnp.float32(scale), jnp.float32(0))
            return d_slots[i, slot_lo] * of_lo + d_slots[i, slot_hi] * of_hi

        late = slice(rows // 2, rows)
        for i, left, right, first_half in (
            (1, gg_t, prob, dv_early),
            (0, qq_t, dscore, dk_early),
        ):
            grads = first_half[...] + jnp.dot(
                left[:, late], right[late, :], preferred_element_type=jnp.float32
            )
            for p in range(slots):
                cols = slice(p * BLK, (p + 1) * BLK)
                d_slots[i, p] = pick(p, grads[:HEAD_SIZE, cols], grads[HEAD_SIZE:, cols])
            for b in range(2):
                at = slice(b * BLK, (b + 1) * BLK)
                mate_send[h, i, 0, at] = partial(i, mate, b).astype(jnp.bfloat16)
                mate_send[h, i, 1, at] = partial(i, cross, b).astype(jnp.bfloat16)
            mate_copy(h, i).start()
            for b in range(2):
                at = slice(b * BLK, (b + 1) * BLK)
                y_part[h, i, at] = partial(i, peer, b)
                own_part[h, i, at] = partial(i, me, b)
        second_stage(h, 1)
        return carry

    lax.fori_loop(0, heads, one_head, 0)
    second_stage(heads - 1, 0)

    dkv_copies = []
    for h in range(heads):
        for i, dst in ((1, dv_hbm), (0, dk_hbm)):
            peer_copy(h, i).wait_recv()
            total = (
                own_part[h, i]
                + mate_recv[h, i, 0].astype(jnp.float32)
                + y_recv[h, i].astype(jnp.float32)
            )
            for b in range(2):
                at = slice(b * BLK, (b + 1) * BLK)
                dkv_buf[h, i, at] = total[at].T.astype(jnp.bfloat16)
            copy = pltpu.make_async_copy(
                dkv_buf.at[h, i], dst.at[:, h * HEAD_SIZE : (h + 1) * HEAD_SIZE], dkv_sem.at[h, i]
            )
            copy.start()
            dkv_copies.append(copy)

    for h in range(heads):
        for i in range(2):
            gather_copy(h, i, me, peer, 0).wait_send()
            gather_copy(h, i, me, mate, 1).wait_send()
            gather_copy(h, i, peer, mate, 2).wait_send()
            mate_copy(h, i).wait_send()
            peer_copy(h, i).wait_send()
        for b in range(2):
            out_copy(h, b, 0).wait()
            out_copy(h, b, 1).wait()
    for copy in dkv_copies:
        copy.wait()


def write_kernel(*refs):
    copies = []
    for i in range(4):
        src, dst = refs[i], refs[4 + i]
        part = src.shape[0] // 4
        for n in range(4):
            at = slice(n * part, (n + 1) * part)
            copies.append(pltpu.make_async_copy(src.at[at], dst.at[at], refs[8].at[i, n]))
    for copy in copies:
        copy.start()
    for copy in copies:
        copy.wait()


def per_device_fused(query_rows, key_rows, stored_value_rows, out_grad, block_table, pattern):
    blocks = pattern.shape[0]
    held, kv_width = key_rows.shape
    heads = kv_width // HEAD_SIZE
    groups = query_rows.shape[1] // kv_width
    width = groups * HEAD_SIZE
    rows = groups * BLK
    slots = blocks + 1
    bf16, f32 = jnp.bfloat16, jnp.float32
    vmem, dma = pltpu.VMEM, pltpu.SemaphoreType.DMA
    ctx = blocks // 2
    pair = 2 * HEAD_SIZE
    scratch = [
        vmem((heads, 2, ctx, held, HEAD_SIZE), bf16),
        vmem((2, blocks, BLK, HEAD_SIZE), bf16),
        vmem((2, BLK, heads * width), bf16),
        vmem((2, BLK, heads * width), bf16),
        vmem((heads, 2, BLK, width), bf16),
        vmem((heads, 2, BLK, width), bf16),
        vmem((rows, pair), bf16),
        vmem((rows, pair), bf16),
        vmem((pair, rows), bf16),
        vmem((pair, rows), bf16),
        vmem((ROWS_CHUNK, pair), bf16),
        vmem((ROWS_CHUNK, pair), bf16),
        vmem((slots * BLK, pair), bf16),
        vmem((slots * BLK, pair), bf16),
        vmem((pair, slots * BLK), bf16),
        vmem((pair, slots * BLK), bf16),
        vmem((2, ROWS_CHUNK, slots * BLK), f32),
        vmem((2, ROWS_CHUNK, slots * BLK), f32),
        vmem((pair, slots * BLK), f32),
        vmem((pair, slots * BLK), f32),
        vmem((rows, slots * BLK), bf16),
        vmem((rows, slots * BLK), bf16),
        vmem((2, rows, HEAD_SIZE), bf16),
        vmem((2, rows, HEAD_SIZE), bf16),
        vmem((2, slots, HEAD_SIZE, BLK), f32),
        vmem((heads, 2, held, HEAD_SIZE), f32),
        vmem((heads, 2, held, HEAD_SIZE), f32),
        vmem((heads, 2, 2, held, HEAD_SIZE), bf16),
        vmem((heads, 2, 2, held, HEAD_SIZE), bf16),
        vmem((heads, 2, held, HEAD_SIZE), bf16),
        vmem((heads, 2, held, HEAD_SIZE), bf16),
        vmem((heads, 2, held, HEAD_SIZE), bf16),
        dma((2, 2)),
        dma((heads, 2)),
        dma((heads, 2, 2)),
        dma((heads, 2)),
        dma((heads, 2, 3)),
        dma((heads, 2, 3)),
        dma((heads, 2, 2)),
        dma((heads, 2, 2)),
    ]
    smem = pl.BlockSpec(memory_space=pltpu.SMEM)
    hbm = pl.BlockSpec(memory_space=pltpu.HBM)
    out_shapes = (query_rows.shape, query_rows.shape, key_rows.shape, key_rows.shape)
    results = pl.pallas_call(
        functools.partial(fused_kernel, heads, groups, blocks),
        out_shape=tuple(jax.ShapeDtypeStruct(shape, bf16) for shape in out_shapes),
        in_specs=[smem, smem, hbm, hbm, hbm, hbm],
        out_specs=(hbm, hbm, hbm, hbm),
        scratch_shapes=scratch,
        compiler_params=pltpu.CompilerParams(
            collective_id=0, has_side_effects=True, vmem_limit_bytes=56 * 1024 * 1024
        ),
        cost_estimate=pl.CostEstimate(
            flops=12 * heads * rows * pair * slots * BLK,
            bytes_accessed=8 * query_rows.size + 8 * key_rows.size,
            transcendentals=heads * rows * slots * BLK,
        ),
    )(block_table.T, pattern, query_rows, key_rows, stored_value_rows, out_grad)
    return pl.pallas_call(
        write_kernel,
        out_shape=tuple(jax.ShapeDtypeStruct(shape, bf16) for shape in out_shapes),
        in_specs=[hbm] * 4,
        out_specs=(hbm,) * 4,
        scratch_shapes=[dma((4, 4))],
        compiler_params=pltpu.CompilerParams(vmem_limit_bytes=56 * 1024 * 1024),
    )(*results)


def solution(mesh):
    row_spec = P(("dp", "ctx"), "head")
    in_specs = (row_spec, row_spec, row_spec, row_spec, P("dp", None), P("dp", None))
    out_specs = (row_spec, row_spec, row_spec, row_spec)

    def per_device(query_rows, key_rows, stored_value_rows, out_grad, block_table, pattern):
        fits = mesh.shape["ctx"] == 4 and block_table.shape == (4, 2)
        body = per_device_fused if fits else per_device_wide
        return body(query_rows, key_rows, stored_value_rows, out_grad, block_table, pattern)

    return jax.shard_map(
        per_device, mesh=mesh, in_specs=in_specs, out_specs=out_specs, check_vma=False
    )
```

```python
import functools

import jax
import jax.numpy as jnp
from jax import lax
from jax.experimental import pallas as pl
from jax.experimental.pallas import tpu as pltpu
from jax.sharding import PartitionSpec as P

HEAD_SIZE = 128
BLK = 128
MESH = pl.DeviceIdType.MESH
ROWS_CHUNK = 256
SUB = 32
NEG = -1e30
SCALE = HEAD_SIZE ** (-0.5)
LOG2E = 1.4426950408889634


def slot_layout(block_table, pattern, held_seq):
    blocks = pattern.shape[0]
    slots = pattern.shape[1]
    block_ids = jnp.arange(blocks, dtype=jnp.int32)
    store_seq = block_table.reshape(-1)
    inverse = jnp.sum(
        jnp.where(store_seq[:, None] == block_ids[None, :], block_ids[:, None], 0), axis=0
    )
    onehot = (held_seq[:, None] == block_ids[None, :]).astype(jnp.int32)
    held_pattern = jnp.sum(onehot[:, :, None] * pattern[None, :, :], axis=1)
    key_store = jnp.sum(
        jnp.where(held_pattern[:, :, None] == block_ids[None, None, :], inverse[None, None, :], 0),
        axis=2,
    )
    same = held_pattern[:, :, None] == held_pattern[:, None, :]
    slot_ids = jnp.arange(slots, dtype=jnp.int32)
    before = slot_ids[None, :] < slot_ids[:, None]
    live_slot = jnp.logical_not(jnp.any(same & before[None], axis=2))
    inner = jnp.arange(BLK, dtype=jnp.int32)
    query_pos = held_seq[:, None] * BLK + inner[None, :]
    key_pos = held_pattern[:, :, None] * BLK + inner[None, None, :]
    allowed = live_slot[:, None, :, None] & (key_pos[:, None, :, :] <= query_pos[:, :, None, None])
    return (key_store, allowed)


def attend_tiles(query_held, grad_held, key_tiles, value_tiles, allowed):
    scaling = HEAD_SIZE ** (-0.5)
    scores = (
        jnp.einsum("biagd,bjkad->bagijk", query_held, key_tiles, preferred_element_type=jnp.float32)
        * scaling
    )
    scores = jnp.where(allowed[:, None, None], scores, -jnp.inf)
    row_max = jnp.max(scores, axis=(4, 5), keepdims=True)
    row_sum = jnp.sum(jnp.exp(scores - row_max), axis=(4, 5), keepdims=True)
    log_total = row_max + jnp.log(row_sum)
    prob_full = jnp.exp(scores - log_total)
    prob_low = prob_full.astype(jnp.bfloat16)
    attended_wide = jnp.einsum(
        "bagijk,bjkad->biagd", prob_low, value_tiles, preferred_element_type=jnp.float32
    )
    attended = attended_wide.astype(jnp.bfloat16)
    row_dot = jnp.sum(grad_held.astype(jnp.float32) * attended_wide, axis=-1)
    row_dot = jnp.transpose(row_dot, (0, 2, 3, 1))[..., None, None]
    grad_prob = jnp.einsum(
        "biagd,bjkad->bagijk", grad_held, value_tiles, preferred_element_type=jnp.float32
    )
    grad_score = (prob_full * (grad_prob - row_dot) * scaling).astype(jnp.bfloat16)
    query_grad = jnp.einsum(
        "bagijk,bjkad->biagd", grad_score, key_tiles, preferred_element_type=jnp.float32
    ).astype(jnp.bfloat16)
    key_grads = jnp.einsum(
        "bagijk,biagd->bjkad", grad_score, query_held, preferred_element_type=jnp.float32
    )
    value_grads = jnp.einsum(
        "bagijk,biagd->bjkad", prob_low, grad_held, preferred_element_type=jnp.float32
    )
    return (attended, query_grad, key_grads, value_grads)


def per_device_wide(query_rows, key_rows, stored_value_rows, out_grad, block_table, pattern):
    ctx_index = lax.axis_index("ctx")
    per_dev = block_table.shape[1]
    blocks = pattern.shape[0]
    kv_local = key_rows.shape[1] // HEAD_SIZE
    groups = query_rows.shape[1] // key_rows.shape[1]
    held_rows = per_dev * BLK
    held_seq = lax.dynamic_index_in_dim(block_table, ctx_index, 0, keepdims=False)
    key_store, allowed = slot_layout(block_table, pattern, held_seq)
    key_all, value_all = (
        lax.all_gather(key_rows, "ctx", axis=0, tiled=True),
        lax.all_gather(stored_value_rows, "ctx", axis=0, tiled=True),
    )
    key_blocks = key_all.reshape(blocks, BLK, kv_local, HEAD_SIZE)
    value_blocks = value_all.reshape(blocks, BLK, kv_local, HEAD_SIZE)
    key_tiles = key_blocks[key_store]
    value_tiles = value_blocks[key_store]
    query_held = query_rows.reshape(per_dev, BLK, kv_local, groups, HEAD_SIZE)
    grad_held = out_grad.reshape(per_dev, BLK, kv_local, groups, HEAD_SIZE)
    attended, query_grad, key_grads, value_grads = attend_tiles(
        query_held, grad_held, key_tiles, value_tiles, allowed
    )
    flat_slots = key_store.reshape(-1)

    def scattered(grads):
        partial = (
            jnp.zeros((blocks, BLK, kv_local, HEAD_SIZE), jnp.float32)
            .at[flat_slots]
            .add(grads.reshape(-1, BLK, kv_local, HEAD_SIZE))
        )
        return lax.psum_scatter(
            partial.reshape(blocks * BLK, -1).astype(jnp.bfloat16),
            "ctx",
            scatter_dimension=0,
            tiled=True,
        ).astype(jnp.bfloat16)

    return (
        attended.reshape(held_rows, -1),
        query_grad.reshape(held_rows, -1),
        scattered(key_grads),
        scattered(value_grads),
    )


def fused_kernel(
    heads, groups, blocks,
    bt_ref, pat_ref, q_hbm, k_hbm, v_hbm, g_hbm,
    att_hbm, dq_hbm, dk_hbm, dv_hbm,
    kv_all, kv_now, q_buf, g_buf, att_buf, dq_buf,
    qq, gg, qq_t, gg_t, q_scaled, g_scaled, key_slots, value_slots, key_t, value_t, s_buf, d_buf, dv_early, dk_early, prob, dscore, att_now, dq_now,
    d_slots, own_part, y_part, mate_send, mate_recv, y_send, y_recv, dkv_buf,
    load_sem, kv_sem, out_sem, dkv_sem, gather_send, gather_recv, red_send, red_recv,
):
    slots = blocks + 1
    half = blocks // 2
    width = groups * HEAD_SIZE
    rows = groups * BLK
    me = lax.axis_index("ctx")
    core, y = me % 2, me // 2
    mate = y * 2 + (1 - core)
    peer = (1 - y) * 2 + core
    cross = (1 - y) * 2 + (1 - core)

    kv_loads = []
    for h in range(heads):
        for i, ref in enumerate((k_hbm, v_hbm)):
            copy = pltpu.make_async_copy(
                ref.at[:, h * HEAD_SIZE : (h + 1) * HEAD_SIZE], kv_all.at[h, i, me], kv_sem.at[h, i]
            )
            copy.start()
            kv_loads.append(copy)
    loads = []
    for i, (src, dst) in enumerate(((q_hbm, q_buf), (g_hbm, g_buf))):
        for b in range(2):
            copy = pltpu.make_async_copy(
                src.at[b * BLK : (b + 1) * BLK], dst.at[b], load_sem.at[i, b]
            )
            copy.start()
            loads.append(copy)

    barrier = pltpu.get_barrier_semaphore()
    for other in (mate, peer):
        pl.semaphore_signal(barrier, inc=1, device_id={"ctx": other}, device_id_type=MESH)
    pl.semaphore_wait(barrier, 2)

    def gather_copy(h, i, source, target, kind):
        return pltpu.make_async_remote_copy(
            src_ref=kv_all.at[h, i, source],
            dst_ref=kv_all.at[h, i, source],
            send_sem=gather_send.at[h, i, kind],
            recv_sem=gather_recv.at[h, i, kind],
            device_id={"ctx": target},
            device_id_type=MESH,
        )

    def gather_arrival(h, i, source, kind):
        return gather_copy(h, i, source, mate, kind)

    def mate_copy(h, i):
        return pltpu.make_async_remote_copy(
            src_ref=mate_send.at[h, i],
            dst_ref=mate_recv.at[h, i],
            send_sem=red_send.at[h, 0, i],
            recv_sem=red_recv.at[h, 0, i],
            device_id={"ctx": mate},
            device_id_type=MESH,
        )

    def peer_copy(h, i):
        return pltpu.make_async_remote_copy(
            src_ref=y_send.at[h, i],
            dst_ref=y_recv.at[h, i],
            send_sem=red_send.at[h, 1, i],
            recv_sem=red_recv.at[h, 1, i],
            device_id={"ctx": peer},
            device_id_type=MESH,
        )

    def out_copy(h, b, i):
        buf, dst = ((att_buf, att_hbm), (dq_buf, dq_hbm))[i]
        return pltpu.make_async_copy(
            buf.at[h, b],
            dst.at[b * BLK : (b + 1) * BLK, pl.ds(pl.multiple_of(h * width, width), width)],
            out_sem.at[h, b, i],
        )

    for h in range(heads):
        for i in range(2):
            kv_loads[2 * h + i].wait()
            gather_copy(h, i, me, peer, 0).start()
            gather_copy(h, i, me, mate, 1).start()

    seq0, seq1 = bt_ref[0, me], bt_ref[1, me]
    lo, hi = jnp.minimum(seq0, seq1), jnp.maximum(seq0, seq1)
    at_lo = jnp.where(seq0 > seq1, 1, 0)
    at_hi = 1 - at_lo
    table = [bt_ref[g % 2, g // 2] for g in range(blocks)]
    homes, biases, is_lo = [], [], []
    for p in range(slots):
        if p == 0:
            mine, key_seq, query_seq = None, lo, lo
        elif p >= half:
            mine, key_seq, query_seq = None, p - lo - 1, hi
        else:
            mine = p <= lo
            key_seq = jnp.where(mine, lo - p, p - lo - 1)
            query_seq = jnp.where(mine, lo, hi)
        home = jnp.int32(0)
        for g in range(blocks):
            home = jnp.where(table[g] == key_seq, g, home)
        homes.append(home)
        is_lo.append(mine)
        if p in (0, slots - 1):
            biases.append(None)
        else:
            hits = jnp.int32(0)
            for j in range(pat_ref.shape[1]):
                hits = hits + jnp.where(pat_ref[query_seq, j] == key_seq, 1, 0)
            biases.append(jnp.where(hits > 0, jnp.float32(0), jnp.float32(NEG)))
    bias_lo = [None if m is None else jnp.where(m, x, NEG) for m, x in zip(is_lo, biases)]
    bias_hi = [None if m is None else jnp.where(m, NEG, x) for m, x in zip(is_lo, biases)]
    in_lo = [None if m is None else jnp.where(m, jnp.float32(1), jnp.float32(0)) for m in is_lo]

    zeros = jnp.zeros((BLK, HEAD_SIZE), jnp.bfloat16)
    for ref, ref_t in ((key_slots, key_t), (value_slots, value_t)):
        for p in range(slots):
            at = slice(p * BLK, (p + 1) * BLK)
            if p == 0:
                ref[at, HEAD_SIZE:] = zeros
                ref_t[HEAD_SIZE:, at] = zeros
            elif p >= half:
                ref[at, :HEAD_SIZE] = zeros
                ref_t[:HEAD_SIZE, at] = zeros

    for copy in loads:
        copy.wait()

    def forward(h, i):
        gather_arrival(h, i, peer, 0).wait_recv()
        gather_copy(h, i, peer, mate, 2).start()

    def second_stage(h, i):
        mate_copy(h, i).wait_recv()
        y_send[h, i] = (y_part[h, i] + mate_recv[h, i, 1].astype(jnp.float32)).astype(jnp.bfloat16)
        peer_copy(h, i).start()

    forward(0, 0)
    forward(0, 1)

    def one_head(h, carry):
        first = pl.multiple_of(h * width, width)
        for src, dst in ((q_buf, qq), (g_buf, gg)):
            for g in range(groups):
                cols = pl.ds(pl.multiple_of(first + g * HEAD_SIZE, HEAD_SIZE), HEAD_SIZE)
                for part, at in ((0, at_lo), (1, at_hi)):
                    tile = src[at, :, cols]
                    dst[g * BLK : (g + 1) * BLK, part * HEAD_SIZE : (part + 1) * HEAD_SIZE] = tile

        for i in range(2):
            gather_arrival(h, i, mate, 1).wait_recv()
            gather_arrival(h, i, cross, 2).wait_recv()
        for i in range(2):
            for c in range(blocks // 2):
                for b in range(2):
                    kv_now[i, c * 2 + b] = kv_all[h, i, c, b * BLK : (b + 1) * BLK]
        for i, (ref, ref_t) in enumerate(((key_slots, key_t), (value_slots, value_t))):
            for p in range(slots):
                tile = kv_now[i, homes[p]]
                tile_t = tile.T
                at = slice(p * BLK, (p + 1) * BLK)
                if p == 0:
                    ref[at, :HEAD_SIZE] = tile
                    ref_t[:HEAD_SIZE, at] = tile_t
                elif p >= half:
                    ref[at, HEAD_SIZE:] = tile
                    ref_t[HEAD_SIZE:, at] = tile_t
                else:
                    for target, index, value in (
                        (ref, (at, slice(0, HEAD_SIZE)), tile),
                        (ref_t, (slice(0, HEAD_SIZE), at), tile_t),
                    ):
                        wide = value.astype(jnp.float32)
                        target[index] = (wide * in_lo[p]).astype(jnp.bfloat16)
                    for target, index, value in (
                        (ref, (at, slice(HEAD_SIZE, None)), tile),
                        (ref_t, (slice(HEAD_SIZE, None), at), tile_t),
                    ):
                        wide = value.astype(jnp.float32)
                        target[index] = (wide * (1.0 - in_lo[p])).astype(jnp.bfloat16)

        def matmuls(c):
            at = slice(c * ROWS_CHUNK, (c + 1) * ROWS_CHUNK)
            s_buf[c % 3] = jnp.dot(qq[at, :], key_t[...], preferred_element_type=jnp.float32)
            d_buf[c % 3] = jnp.dot(gg[at, :], value_t[...], preferred_element_type=jnp.float32)

        def pick(p, of_lo, of_hi):
            if p == 0:
                return of_lo
            if p >= half:
                return of_hi
            return jnp.where(is_lo[p], of_lo, of_hi)

        def softmax(c, r):
            rows_at = slice(c * ROWS_CHUNK + r, c * ROWS_CHUNK + r + SUB)
            inner = slice(r, r + SUB)
            row = lax.broadcasted_iota(jnp.int32, (SUB, BLK), 0) + (c * ROWS_CHUNK + r) % BLK
            col = lax.broadcasted_iota(jnp.int32, (SUB, BLK), 1)
            tiles = [s_buf[c % 3, inner, p * BLK : (p + 1) * BLK] for p in range(slots)]
            for p in (0, slots - 1):
                tiles[p] = jnp.where(col <= row, tiles[p], NEG)
            max_lo, max_hi = tiles[0], tiles[slots - 1]
            for p in range(1, slots - 1):
                if p < half:
                    max_lo = jnp.maximum(max_lo, tiles[p] + bias_lo[p])
                    max_hi = jnp.maximum(max_hi, tiles[p] + bias_hi[p])
                else:
                    max_hi = jnp.maximum(max_hi, tiles[p] + biases[p])
            max_lo = jnp.max(max_lo, axis=1, keepdims=True)
            max_hi = jnp.max(max_hi, axis=1, keepdims=True)
            sum_lo = sum_hi = None
            for p in range(slots):
                top = pick(p, max_lo, max_hi)
                if biases[p] is not None:
                    top = top - biases[p]
                tile = jnp.exp2((tiles[p] - top) * (SCALE * LOG2E))
                s_buf[c % 3, inner, p * BLK : (p + 1) * BLK] = tile
                prob[rows_at, p * BLK : (p + 1) * BLK] = tile.astype(jnp.bfloat16)
                if p == 0:
                    sum_lo = tile
                elif p < half:
                    sum_lo = sum_lo + jnp.where(is_lo[p], tile, 0.0)
                    part = jnp.where(is_lo[p], 0.0, tile)
                    sum_hi = part if sum_hi is None else sum_hi + part
                else:
                    sum_hi = tile if sum_hi is None else sum_hi + tile
            inv_lo = 1.0 / jnp.sum(sum_lo, axis=1, keepdims=True)
            inv_hi = 1.0 / jnp.sum(sum_hi, axis=1, keepdims=True)
            for src, dst in ((qq, q_scaled), (gg, g_scaled)):
                for cols, inv in ((slice(0, HEAD_SIZE), inv_lo), (slice(HEAD_SIZE, None), inv_hi)):
                    dst[c % 2, inner, cols] = (src[rows_at, cols].astype(jnp.float32) * inv).astype(
                        jnp.bfloat16
                    )
            return inv_lo, inv_hi

        def all_softmax(c):
            return [softmax(c, r) for r in range(0, ROWS_CHUNK, SUB)]

        def attend(c):
            at = slice(c * ROWS_CHUNK, (c + 1) * ROWS_CHUNK)
            return jnp.dot(prob[at, :], value_slots[...], preferred_element_type=jnp.float32)

        def score_grads(c, wide, inverses):
            at = slice(c * ROWS_CHUNK, (c + 1) * ROWS_CHUNK)
            for src, dst in ((q_scaled, qq_t), (g_scaled, gg_t)):
                dst[:, at] = src[c % 2].T
            for n, (inv_lo, inv_hi) in enumerate(inverses):
                inner = slice(n * SUB, (n + 1) * SUB)
                rows_at = slice(c * ROWS_CHUNK + n * SUB, c * ROWS_CHUNK + (n + 1) * SUB)
                of_lo = wide[inner, :HEAD_SIZE] * inv_lo
                of_hi = wide[inner, HEAD_SIZE:] * inv_hi
                att_now[0, rows_at, :] = of_lo.astype(jnp.bfloat16)
                att_now[1, rows_at, :] = of_hi.astype(jnp.bfloat16)
                grad = gg[rows_at, :].astype(jnp.float32)
                dot_lo = jnp.sum(of_lo * grad[:, :HEAD_SIZE], axis=1, keepdims=True)
                dot_hi = jnp.sum(of_hi * grad[:, HEAD_SIZE:], axis=1, keepdims=True)
                for p in range(slots):
                    cols = slice(p * BLK, (p + 1) * BLK)
                    dscore[rows_at, cols] = (
                        s_buf[c % 3, inner, cols]
                        * (d_buf[c % 3, inner, cols] - pick(p, dot_lo, dot_hi))
                    ).astype(jnp.bfloat16)

        def query_grads(c, inverses):
            at = slice(c * ROWS_CHUNK, (c + 1) * ROWS_CHUNK)
            dq = jnp.dot(dscore[at, :], key_slots[...], preferred_element_type=jnp.float32)
            for n, (inv_lo, inv_hi) in enumerate(inverses):
                inner = slice(n * SUB, (n + 1) * SUB)
                rows_at = slice(c * ROWS_CHUNK + n * SUB, c * ROWS_CHUNK + (n + 1) * SUB)
                dq_now[0, rows_at, :] = (dq[inner, :HEAD_SIZE] * (inv_lo * SCALE)).astype(
                    jnp.bfloat16
                )
                dq_now[1, rows_at, :] = (dq[inner, HEAD_SIZE:] * (inv_hi * SCALE)).astype(
                    jnp.bfloat16
                )

        chunks = rows // ROWS_CHUNK
        early = slice(0, rows // 2)
        matmuls(0)
        matmuls(1)
        inverses = all_softmax(0)
        for c in range(chunks):
            wide = attend(c)
            if c == chunks // 2:
                dv_early[...] = jnp.dot(
                    gg_t[:, early], prob[early, :], preferred_element_type=jnp.float32
                )
            later = all_softmax(c + 1) if c + 1 < chunks else None
            if c + 2 < chunks:
                matmuls(c + 2)
            if c == chunks - 1:
                dk_early[...] = jnp.dot(
                    qq_t[:, early], dscore[early, :], preferred_element_type=jnp.float32
                )
            score_grads(c, wide, inverses)
            query_grads(c, inverses)
            inverses = later

        @pl.when(h < heads - 1)
        def _():
            forward(h + 1, 0)
            forward(h + 1, 1)

        @pl.when(h > 0)
        def _():
            second_stage(h - 1, 0)

        for b in range(2):
            from_now = jnp.where(at_lo == b, 0, 1)
            for g in range(groups):
                cols = slice(g * HEAD_SIZE, (g + 1) * HEAD_SIZE)
                att_buf[h, b, :, cols] = att_now[from_now, g * BLK : (g + 1) * BLK, :]
                dq_buf[h, b, :, cols] = dq_now[from_now, g * BLK : (g + 1) * BLK, :]
            out_copy(h, b, 0).start()
            out_copy(h, b, 1).start()

        def partial(i, target, b):
            seq = bt_ref[b, target]
            slot_lo = jnp.maximum(lo - seq, 0)
            slot_hi = jnp.minimum(lo + 1 + seq, slots - 1)
            scale = SCALE if i == 0 else 1.0
            of_lo = jnp.where(seq <= lo, jnp.float32(scale), jnp.float32(0))
            of_hi = jnp.where(seq <= hi, jnp.float32(scale), jnp.float32(0))
            return d_slots[i, slot_lo] * of_lo + d_slots[i, slot_hi] * of_hi

        late = slice(rows // 2, rows)
        for i, left, right, first_half in (
            (1, gg_t, prob, dv_early),
            (0, qq_t, dscore, dk_early),
        ):
            grads = first_half[...] + jnp.dot(
                left[:, late], right[late, :], preferred_element_type=jnp.float32
            )
            for p in range(slots):
                cols = slice(p * BLK, (p + 1) * BLK)
                d_slots[i, p] = pick(p, grads[:HEAD_SIZE, cols], grads[HEAD_SIZE:, cols])
            for b in range(2):
                at = slice(b * BLK, (b + 1) * BLK)
                mate_send[h, i, 0, at] = partial(i, mate, b).astype(jnp.bfloat16)
                mate_send[h, i, 1, at] = partial(i, cross, b).astype(jnp.bfloat16)
            mate_copy(h, i).start()
            for b in range(2):
                at = slice(b * BLK, (b + 1) * BLK)
                y_part[h, i, at] = partial(i, peer, b)
                own_part[h, i, at] = partial(i, me, b)
        second_stage(h, 1)
        return carry

    lax.fori_loop(0, heads, one_head, 0)
    second_stage(heads - 1, 0)

    dkv_copies = []
    for h in range(heads):
        for i, dst in ((1, dv_hbm), (0, dk_hbm)):
            peer_copy(h, i).wait_recv()
            total = (
                own_part[h, i]
                + mate_recv[h, i, 0].astype(jnp.float32)
                + y_recv[h, i].astype(jnp.float32)
            )
            for b in range(2):
                at = slice(b * BLK, (b + 1) * BLK)
                dkv_buf[h, i, at] = total[at].T.astype(jnp.bfloat16)
            copy = pltpu.make_async_copy(
                dkv_buf.at[h, i], dst.at[:, h * HEAD_SIZE : (h + 1) * HEAD_SIZE], dkv_sem.at[h, i]
            )
            copy.start()
            dkv_copies.append(copy)

    for h in range(heads):
        for i in range(2):
            gather_copy(h, i, me, peer, 0).wait_send()
            gather_copy(h, i, me, mate, 1).wait_send()
            gather_copy(h, i, peer, mate, 2).wait_send()
            mate_copy(h, i).wait_send()
            peer_copy(h, i).wait_send()
        for b in range(2):
            out_copy(h, b, 0).wait()
            out_copy(h, b, 1).wait()
    for copy in dkv_copies:
        copy.wait()


def write_kernel(*refs):
    reads, writes = [], []
    for i in range(4):
        src, dst, held = refs[i], refs[4 + i], refs[8 + i]
        part = src.shape[0] // 4
        for n in range(4):
            at = slice(n * part, (n + 1) * part)
            reads.append(pltpu.make_async_copy(src.at[at], held.at[at], refs[12].at[i, n]))
            writes.append(pltpu.make_async_copy(held.at[at], dst.at[at], refs[13].at[i, n]))
    for copy in reads:
        copy.start()
    for read, write in zip(reads, writes):
        read.wait()
        write.start()
    for copy in writes:
        copy.wait()


def per_device_fused(query_rows, key_rows, stored_value_rows, out_grad, block_table, pattern):
    blocks = pattern.shape[0]
    held, kv_width = key_rows.shape
    heads = kv_width // HEAD_SIZE
    groups = query_rows.shape[1] // kv_width
    width = groups * HEAD_SIZE
    rows = groups * BLK
    slots = blocks + 1
    bf16, f32 = jnp.bfloat16, jnp.float32
    vmem, dma = pltpu.VMEM, pltpu.SemaphoreType.DMA
    ctx = blocks // 2
    pair = 2 * HEAD_SIZE
    scratch = [
        vmem((heads, 2, ctx, held, HEAD_SIZE), bf16),
        vmem((2, blocks, BLK, HEAD_SIZE), bf16),
        vmem((2, BLK, heads * width), bf16),
        vmem((2, BLK, heads * width), bf16),
        vmem((heads, 2, BLK, width), bf16),
        vmem((heads, 2, BLK, width), bf16),
        vmem((rows, pair), bf16),
        vmem((rows, pair), bf16),
        vmem((pair, rows), bf16),
        vmem((pair, rows), bf16),
        vmem((2, ROWS_CHUNK, pair), bf16),
        vmem((2, ROWS_CHUNK, pair), bf16),
        vmem((slots * BLK, pair), bf16),
        vmem((slots * BLK, pair), bf16),
        vmem((pair, slots * BLK), bf16),
        vmem((pair, slots * BLK), bf16),
        vmem((3, ROWS_CHUNK, slots * BLK), f32),
        vmem((3, ROWS_CHUNK, slots * BLK), f32),
        vmem((pair, slots * BLK), f32),
        vmem((pair, slots * BLK), f32),
        vmem((rows, slots * BLK), bf16),
        vmem((rows, slots * BLK), bf16),
        vmem((2, rows, HEAD_SIZE), bf16),
        vmem((2, rows, HEAD_SIZE), bf16),
        vmem((2, slots, HEAD_SIZE, BLK), f32),
        vmem((heads, 2, held, HEAD_SIZE), f32),
        vmem((heads, 2, held, HEAD_SIZE), f32),
        vmem((heads, 2, 2, held, HEAD_SIZE), bf16),
        vmem((heads, 2, 2, held, HEAD_SIZE), bf16),
        vmem((heads, 2, held, HEAD_SIZE), bf16),
        vmem((heads, 2, held, HEAD_SIZE), bf16),
        vmem((heads, 2, held, HEAD_SIZE), bf16),
        dma((2, 2)),
        dma((heads, 2)),
        dma((heads, 2, 2)),
        dma((heads, 2)),
        dma((heads, 2, 3)),
        dma((heads, 2, 3)),
        dma((heads, 2, 2)),
        dma((heads, 2, 2)),
    ]
    smem = pl.BlockSpec(memory_space=pltpu.SMEM)
    hbm = pl.BlockSpec(memory_space=pltpu.HBM)
    out_shapes = (query_rows.shape, query_rows.shape, key_rows.shape, key_rows.shape)
    results = pl.pallas_call(
        functools.partial(fused_kernel, heads, groups, blocks),
        out_shape=tuple(jax.ShapeDtypeStruct(shape, bf16) for shape in out_shapes),
        in_specs=[smem, smem, hbm, hbm, hbm, hbm],
        out_specs=(hbm, hbm, hbm, hbm),
        scratch_shapes=scratch,
        compiler_params=pltpu.CompilerParams(
            collective_id=0, has_side_effects=True, vmem_limit_bytes=56 * 1024 * 1024
        ),
        cost_estimate=pl.CostEstimate(
            flops=12 * heads * rows * pair * slots * BLK,
            bytes_accessed=8 * query_rows.size + 8 * key_rows.size,
            transcendentals=heads * rows * slots * BLK,
        ),
    )(block_table.T, pattern, query_rows, key_rows, stored_value_rows, out_grad)
    return pl.pallas_call(
        write_kernel,
        out_shape=tuple(jax.ShapeDtypeStruct(shape, bf16) for shape in out_shapes),
        in_specs=[hbm] * 4,
        out_specs=(hbm,) * 4,
        scratch_shapes=[vmem(shape, bf16) for shape in out_shapes] + [dma((4, 4)), dma((4, 4))],
        compiler_params=pltpu.CompilerParams(vmem_limit_bytes=56 * 1024 * 1024),
    )(*results)


def solution(mesh):
    row_spec = P(("dp", "ctx"), "head")
    in_specs = (row_spec, row_spec, row_spec, row_spec, P("dp", None), P("dp", None))
    out_specs = (row_spec, row_spec, row_spec, row_spec)

    def per_device(query_rows, key_rows, stored_value_rows, out_grad, block_table, pattern):
        fits = mesh.shape["ctx"] == 4 and block_table.shape == (4, 2)
        body = per_device_fused if fits else per_device_wide
        return body(query_rows, key_rows, stored_value_rows, out_grad, block_table, pattern)

    return jax.shard_map(
        per_device, mesh=mesh, in_specs=in_specs, out_specs=out_specs, check_vma=False
    )
```
